128 devices in a mesh: bx: 16 (over y, x), by: 8 (over z, core).
Axes of the slice: x: 4, y: 4, z: 4, core: 2. Of those that a mesh axis runs over, the one named last changes fastest.
Arguments:
- currents: bfloat16 [128, 128, 128, 128], P(('bx', 'by')), may hold values from -6 to 6
- counts: int32 [128, 128], P(('bx', 'by')), may hold values from 0 to 128, as said below
- box_of: int32 [128, 128, 128], P(('bx', 'by')), may hold values from 0 to 15
- source_map: bfloat16 [128, 128], replicated, may hold values from -0.02734375 to 0.02734375
- phases: float32 [5, 64, 1048576], P(None, None, ('bx', 'by')), may hold values from -3.140625 to 3.140625
- trans: bfloat16 [4, 2, 2, 128, 128], replicated, may hold values from -0.375 to 0.375
Outputs:
- far_field: bfloat16 [128, 1048576], P(None, ('bx', 'by'))
The draws below stay inside these ranges and needn't reach their ends.
Inputs may be any that keep to these rules, and one draw needn't show every extreme that they name: counts[s, d] <= 128; in every draw some owner receives exactly 128 rows from every partition.
All inputs are finite; a program needn't handle non-finite values.
Results may differ from the reference program's by a relative error of at most 0.012.
Values may be sent and summed in bfloat16 or wider, within the bound.
No kernel may reach another device: no remote copies, remote signals or barrier semaphores. Data moves between devices by JAX's collectives and lax.ppermute only.
A program may use at most 64 MiB of HBM per device.

```python
import math
import jax
import jax.numpy as jnp
from jax import lax

P_SIZE = 64
CAP = 128
BOXES = 16
DIRS = 512
LEVELS = 4
OWNERS = 128
ROWS = 8192
N_BY = 8


def draw_counts(key, part):
    key = jax.random.fold_in(key, 11)
    first, second, third = jax.random.split(key, 3)
    source = jnp.arange(OWNERS, dtype=jnp.int32)[:, None]
    target = jnp.arange(OWNERS, dtype=jnp.int32)[None, :]
    offset = jnp.bitwise_xor(source, target)
    near = (offset < 4) | (offset == OWNERS // 8) | (offset == OWNERS // 4) | (offset == OWNERS // 2) | (offset == OWNERS // 2 + 1)
    heavy = jax.random.randint(first, (OWNERS, OWNERS), CAP // 2, CAP + 1)
    light = jax.random.randint(third, (OWNERS, OWNERS), CAP // 8, CAP // 2 + 1)
    chosen = jax.random.randint(second, (), 0, OWNERS)
    counts = jnp.where(near, heavy, light)
    counts = jnp.where(target == chosen, CAP, counts)
    return counts.astype(jnp.int32)


def set_ends(array, own_key, low, largest):
    place = [jax.random.randint(jax.random.fold_in(own_key, axis), (), 0, length) for axis, length in enumerate(array.shape)]
    main_axis = array.shape.index(max(array.shape))
    next_to = place[:main_axis] + [(place[main_axis] + 1) % array.shape[main_axis]] + place[main_axis + 1:]
    return array.at[tuple(place)].set(low).at[tuple(next_to)].set(largest)


def shard_levels(rng, shape, shards, smallest, top_value):
    def one(axis_at, shards_of):
        heights = jax.random.uniform(jax.random.fold_in(jax.random.fold_in(rng, 6), axis_at), (shards_of,), jnp.float32, smallest / len(shards), top_value / len(shards))
        return jnp.repeat(jnp.exp(heights), shape[axis_at] // shards_of).reshape((-1,) + (1,) * (len(shape) - axis_at - 1))

    loudness = one(*shards[0])
    for cut in shards[1:]:
        loudness = loudness * one(*cut)
    return loudness


def noise(own_key, shape, deviation, most, pieces=(), held_as=jnp.bfloat16):
    gain = shard_levels(own_key, shape, pieces, -0.22, 0.18) if pieces else 1.0
    entries = jax.random.normal(own_key, shape, jnp.float32) * deviation * gain
    return jnp.minimum(jnp.maximum(entries, -most), most).astype(held_as)


def setup_inputs(seed: int = 0) -> dict:
    splits = jax.random.split(jax.random.key(seed), 7)
    currents = noise(splits[0], (OWNERS, OWNERS, CAP, 2 * P_SIZE), 1.0, 6.0, ((0, 128),))
    counts = draw_counts(jax.random.fold_in(splits[6], 71), 0)
    box_of = set_ends(jax.random.randint(splits[2], (OWNERS, OWNERS, CAP), 0, BOXES), jax.random.fold_in(splits[2], 1), 0, BOXES - 1).astype(jnp.int32)
    source_map = noise(splits[3], (2 * P_SIZE, 2 * P_SIZE), (2 * P_SIZE * OWNERS * CAP // (3 * BOXES)) ** -0.5, 0.02734375)
    phases = jnp.clip(jax.random.uniform(splits[4], (LEVELS + 1, P_SIZE, ROWS * OWNERS), jnp.float32, -3.140625, 3.140625), -3.140625, 3.140625)
    trans = noise(splits[5], (LEVELS, 2, 2, 2 * P_SIZE, 2 * P_SIZE), (4 * P_SIZE) ** -0.5, 0.375)
    return {"currents": currents, "counts": counts, "box_of": box_of, "source_map": source_map, "phases": phases, "trans": trans}


def rotate(z, angle):
    half = z.shape[-2] // 2
    re = z[..., :half, :]
    im = z[..., half:, :]
    cosine = jnp.cos(angle)
    sine = jnp.sin(angle)
    return jnp.concatenate([re * cosine - im * sine, re * sine + im * cosine], axis=-2)


def reference(currents, counts, box_of, source_map, phases, trans):
    owners = counts.shape[0]
    slots = jnp.arange(CAP, dtype=jnp.int32)
    live = slots[None, None, :] < counts[:, :, None]
    tag = jnp.where(live, box_of, -1)
    labels = jnp.arange(BOXES, dtype=jnp.int32)

    def per_owner(dest):
        onehot = (tag[:, dest, :, None] == labels).astype(jnp.float32)
        rows = currents[:, dest].astype(jnp.float32)
        return jnp.einsum("scb,scq->bq", onehot, rows)

    box_sum = lax.map(per_owner, jnp.arange(owners, dtype=jnp.int32)).astype(jnp.bfloat16)
    expansion = jnp.einsum("dbq,qo->dbo", box_sum.astype(jnp.float32), source_map.astype(jnp.float32))
    width = expansion.shape[-1]
    spread = jnp.broadcast_to(jnp.transpose(expansion, (0, 2, 1))[:, :, :, None], (owners, width, BOXES, DIRS))
    spread = spread.reshape(owners, width, BOXES * DIRS)
    angles = phases.reshape(LEVELS + 1, P_SIZE, owners, BOXES * DIRS).transpose(2, 0, 1, 3)
    state = rotate(spread, angles[:, 0]).astype(jnp.bfloat16)
    by_bits = int(math.log2(N_BY))
    device = jnp.arange(owners, dtype=jnp.int32)
    for level in range(LEVELS):
        bit = level // 2
        shift = bit + by_bits if level % 2 == 0 else bit
        partner = jnp.bitwise_xor(device, 1 << shift)
        beta = jnp.bitwise_and(jnp.right_shift(device, shift), 1)
        mats = trans[level].astype(jnp.float32)[beta]
        other = state[partner]
        mixed = jnp.einsum("dio,dir->dor", mats[:, 0], state.astype(jnp.float32))
        mixed = mixed + jnp.einsum("dio,dir->dor", mats[:, 1], other.astype(jnp.float32))
        state = rotate(mixed, angles[:, level + 1]).astype(jnp.bfloat16)
    return jnp.transpose(state, (1, 0, 2)).reshape(width, owners * BOXES * DIRS)
```

```python
import functools

import jax
import jax.numpy as jnp
from jax import lax
from jax.experimental import pallas as pl
from jax.experimental.pallas import tpu as pltpu
from jax.sharding import PartitionSpec as P

BOXES = 16
DIRS = 512
HALF = 64
WIDTH = 128
ROWS = BOXES * DIRS
SPLIT = 4
OWNERS_PER_STEP = 16

TURN = 32767.0 / 3.141592653589793
SIN_HALF = (0.7071043848991394, -0.02945953793823719, 0.0003670926089398563, -2.0290131033107173e-06)
COS_HALF = (
    1.4142135381698608,
    -0.17677636444568634,
    0.003682575887069106,
    -3.061274401261471e-05,
    1.2791403491974052e-07,
)


def horner(terms, square):
    total = jnp.full_like(square, terms[-1])
    for term in terms[-2::-1]:
        total = total * square + term
    return total


def cos_sin(angle):
    square = angle * angle
    sine = horner(SIN_HALF, square) * angle
    cosine = horner(COS_HALF, square)
    return 1.0 - sine * sine, sine * cosine


def turn(re, im, angle):
    cosine, sine = cos_sin(angle)
    top = re * cosine - im * sine
    low = re * sine + im * cosine
    return jnp.concatenate([top, low], axis=0).astype(jnp.bfloat16)


def box_sums_kernel(counts_ref, tag_ref, rows_ref, out_ref):
    first = pl.program_id(0) * OWNERS_PER_STEP
    slot = lax.broadcasted_iota(jnp.int32, (BOXES, WIDTH), 1)
    label = lax.broadcasted_iota(jnp.int32, (BOXES, WIDTH), 0)
    for j in range(OWNERS_PER_STEP):
        live = slot < counts_ref[0, first + j]
        hit = jnp.logical_and(tag_ref[j : j + 1, :] == label, live)
        picks = jnp.where(hit, 1.0, 0.0).astype(jnp.bfloat16)
        out_ref[j] = jnp.dot(picks, rows_ref[j], preferred_element_type=jnp.float32).astype(jnp.bfloat16)


def box_sums(counts, tag, rows):
    owners = rows.shape[0]
    step = OWNERS_PER_STEP
    return pl.pallas_call(
        box_sums_kernel,
        grid=(owners // step,),
        in_specs=[
            pl.BlockSpec(memory_space=pltpu.SMEM),
            pl.BlockSpec((step, WIDTH), lambda i: (i, 0)),
            pl.BlockSpec((step, WIDTH, WIDTH), lambda i: (i, 0, 0)),
        ],
        out_specs=pl.BlockSpec((step, BOXES, WIDTH), lambda i: (i, 0, 0)),
        out_shape=jax.ShapeDtypeStruct((owners, BOXES, WIDTH), jnp.bfloat16),
        name="box_sums",
    )(counts, tag, rows)


def expand_kernel(parts_ref, map_ref, out_ref):
    total = jnp.sum(parts_ref[...].astype(jnp.float32), axis=0)
    out_ref[...] = jnp.dot(total.astype(jnp.bfloat16), map_ref[...], preferred_element_type=jnp.float32)


def expand(parts, source_map):
    return pl.pallas_call(
        expand_kernel,
        out_shape=jax.ShapeDtypeStruct((BOXES, WIDTH), jnp.float32),
        name="expand",
    )(parts, source_map)


def column(x_ref, box):
    row = jnp.broadcast_to(x_ref[pl.ds(box, 1), :], (8, WIDTH))
    return row.T[:, :1]


def first_kernel(start, x_ref, other_x_ref, mats_ref, angle0_ref, other_ref, angle1_ref, out_ref):
    box = start + pl.program_id(0)
    mine = column(x_ref, box)
    state = turn(mine[:HALF], mine[HALF:], angle0_ref[...])
    theirs = column(other_x_ref, box)
    angle = other_ref[...].astype(jnp.int32).astype(jnp.float32) * (1.0 / TURN)
    partner = turn(theirs[:HALF], theirs[HALF:], angle)
    both = jnp.concatenate([state, partner], axis=0)
    mixed = jnp.dot(mats_ref[...], both, preferred_element_type=jnp.float32)
    out_ref[...] = turn(mixed[:HALF], mixed[HALF:], angle1_ref[...])


def first_level(part, x, other_x, mats, phases, other_turns):
    blocks = BOXES // SPLIT
    start = part * blocks
    whole = lambda i: (0, 0)
    return pl.pallas_call(
        functools.partial(first_kernel, start),
        grid=(blocks,),
        in_specs=[
            pl.BlockSpec((BOXES, WIDTH), whole),
            pl.BlockSpec((BOXES, WIDTH), whole),
            pl.BlockSpec((WIDTH, 2 * WIDTH), whole),
            pl.BlockSpec((None, HALF, DIRS), lambda i: (0, 0, start + i)),
            pl.BlockSpec((HALF, DIRS), lambda i: (0, start + i)),
            pl.BlockSpec((None, HALF, DIRS), lambda i: (1, 0, start + i)),
        ],
        out_specs=pl.BlockSpec((WIDTH, DIRS), lambda i: (0, i)),
        out_shape=jax.ShapeDtypeStruct((WIDTH, ROWS // SPLIT), jnp.bfloat16),
        name="first_level",
    )(x, other_x, mats, phases, other_turns, phases)


def level_kernel(state_ref, partner_ref, mats_ref, angle_ref, out_ref):
    both = jnp.concatenate([state_ref[...], partner_ref[...]], axis=0)
    mixed = jnp.dot(mats_ref[...], both, preferred_element_type=jnp.float32)
    out_ref[...] = turn(mixed[:HALF], mixed[HALF:], angle_ref[...])


def last_kernel(state_ref, partner_ref, mats_ref, angle_ref, held_ref, out_ref):
    level_kernel(state_ref, partner_ref, mats_ref, angle_ref, out_ref)


def next_level(part, level, state, partner, mats, phases, held=None):
    blocks = BOXES // SPLIT
    start = part * blocks
    in_specs = [
        pl.BlockSpec((WIDTH, DIRS), lambda i: (0, i)),
        pl.BlockSpec((WIDTH, DIRS), lambda i: (0, i)),
        pl.BlockSpec((WIDTH, 2 * WIDTH), lambda i: (0, 0)),
        pl.BlockSpec((None, HALF, DIRS), lambda i: (level + 1, 0, start + i)),
    ]
    operands = [state, partner, mats, phases]
    last = level == 3
    aliases = {}
    if held is not None:
        in_specs.append(pl.BlockSpec(memory_space=pl.ANY))
        operands.append(held)
        aliases = {4: 0}
    return pl.pallas_call(
        level_kernel if held is None else last_kernel,
        grid=(blocks,),
        in_specs=in_specs,
        out_specs=pl.BlockSpec((WIDTH, DIRS), (lambda i: (0, start + i)) if last else (lambda i: (0, i))),
        out_shape=jax.ShapeDtypeStruct((WIDTH, ROWS if last else ROWS // SPLIT), jnp.bfloat16),
        input_output_aliases=aliases,
        name="level_%d" % level,
    )(*operands)


def swap(value, axis, bit):
    mask = 1 << bit
    return lax.ppermute(value, axis, [(s, s ^ mask) for s in range(lax.axis_size(axis))])


def pick(trans, level, position, bit):
    beta = jnp.bitwise_and(jnp.right_shift(position, bit), 1)
    mats = lax.dynamic_index_in_dim(trans[level], beta, 0, keepdims=False)
    return mats.reshape(2 * WIDTH, WIDTH).T


def per_device(currents, counts, box_of, source_map, phases, trans):
    turns = jnp.round(phases[0] * TURN).astype(jnp.int16)
    other_turns = swap(turns, "bx", 0)
    sums = box_sums(counts, box_of[0], currents[0])
    parts = lax.all_to_all(sums, ("bx", "by"), split_axis=0, concat_axis=0, tiled=True)
    x = expand(parts, source_map)
    other_x = swap(x, "bx", 0)
    bx = lax.axis_index("bx")
    by = lax.axis_index("by")
    mats = [pick(trans, 0, bx, 0), pick(trans, 1, by, 0), pick(trans, 2, bx, 1), pick(trans, 3, by, 1)]
    state = [first_level(p, x, other_x, mats[0], phases, other_turns) for p in range(SPLIT)]
    for level, (axis, bit) in ((1, ("by", 0)), (2, ("bx", 1))):
        state = [next_level(p, level, s, swap(s, axis, bit), mats[level], phases) for p, s in enumerate(state)]
    held = None
    for p, s in enumerate(state):
        held = next_level(p, 3, s, swap(s, "by", 1), mats[3], phases, held)
    return held


def solution(mesh):
    placed = (
        P(("bx", "by"), None, None, None),
        P(("bx", "by"), None),
        P(("bx", "by"), None, None),
        P(),
        P(None, None, ("bx", "by")),
        P(),
    )
    return jax.shard_map(
        per_device, mesh=mesh, in_specs=placed, out_specs=P(None, ("bx", "by")), check_vma=False
    )
```

```python
import functools

import jax
import jax.numpy as jnp
from jax import lax
from jax.experimental import pallas as pl
from jax.experimental.pallas import tpu as pltpu
from jax.sharding import PartitionSpec as P

BOXES = 16
DIRS = 512
HALF = 64
WIDTH = 128
ROWS = BOXES * DIRS
LEVELS = 4
PARTS = (2, 2, 2, 2, 2, 2, 2, 2)
SENDS = (16,)
SPAN = 1024
FETCHES = 4
ALONG = 4
AHEAD = 4
MIB = 1 << 20

TURN = 32767.0 / 3.141592653589793
SIN_HALF = (0.7071043848991394, -0.02945953793823719, 0.0003670926089398563, -2.0290131033107173e-06)
COS_HALF = (
    1.4142135381698608,
    -0.17677636444568634,
    0.003682575887069106,
    -3.061274401261471e-05,
    1.2791403491974052e-07,
)

ANY = pl.BlockSpec(memory_space=pl.ANY)
VMEM = pl.BlockSpec(memory_space=pltpu.VMEM)
SMEM = pl.BlockSpec(memory_space=pltpu.SMEM)


def near(value):
    return pltpu.with_memory_space_constraint(value, pltpu.VMEM)


def far(value):
    return pltpu.with_memory_space_constraint(value, pltpu.HBM)


def limit(mib):
    return pltpu.CompilerParams(vmem_limit_bytes=mib * MIB)


def kernel_call(*args, **kwargs):
    cost = pl.CostEstimate(flops=1000, bytes_accessed=1000, transcendentals=0)
    return pl.pallas_call(*args, cost_estimate=cost, **kwargs)


def place_of(part):
    axis, shift, count = {"core": ("by", 0, 2), "z": ("by", 1, 4), "x": ("bx", 0, 4), "y": ("bx", 2, 4)}[part]
    return lax.rem(lax.div(lax.axis_index(axis).astype(jnp.int32), jnp.int32(1 << shift)), jnp.int32(count))


def horner(terms, square):
    total = jnp.full_like(square, terms[-1])
    for term in terms[-2::-1]:
        total = total * square + term
    return total


def cos_sin(angle):
    square = angle * angle
    sine = horner(SIN_HALF, square) * angle
    cosine = horner(COS_HALF, square)
    return 1.0 - sine * sine, sine * cosine


def turn(re, im, cosine, sine):
    top = re * cosine - im * sine
    low = re * sine + im * cosine
    return jnp.concatenate([top, low], axis=0).astype(jnp.bfloat16)


def encode_kernel(phases_ref, *rest):
    out_refs, (held, sems) = rest[: len(SENDS)], rest[len(SENDS) :]
    copies = []
    for i, n in enumerate(SENDS):
        cols = pl.ds(sum(SENDS[:i]) * DIRS, n * DIRS)
        copies.append(pltpu.make_async_copy(phases_ref.at[0, :, cols], held.at[:, cols], sems.at[i]))
        copies[-1].start()
    for i, n in enumerate(SENDS):
        copies[i].wait()
        cols = pl.ds(sum(SENDS[:i]) * DIRS, n * DIRS)
        out_refs[i][...] = jnp.round(held[:, cols] * TURN).astype(jnp.int32).astype(jnp.int16)


def encode(phases):
    return kernel_call(
        encode_kernel,
        in_specs=[ANY],
        out_specs=[VMEM] * len(SENDS),
        out_shape=[pltpu.VMEM((HALF, n * DIRS), jnp.int16) for n in SENDS],
        scratch_shapes=[pltpu.VMEM((HALF, ROWS), jnp.float32), pltpu.SemaphoreType.DMA((len(SENDS),))],
        compiler_params=limit(8),
        name="encode",
    )(far(phases))


def fetch_kernel(after_ref, phases_ref, out_ref, sems):
    copies = [pltpu.make_async_copy(phases_ref.at[k], out_ref.at[k], sems.at[k]) for k in range(LEVELS + 1)]
    for copy in copies:
        copy.start()
    for copy in copies:
        copy.wait()


def fetch(after, phases):
    return kernel_call(
        fetch_kernel,
        in_specs=[ANY, ANY],
        out_specs=VMEM,
        out_shape=pltpu.VMEM(phases.shape, jnp.float32),
        scratch_shapes=[pltpu.SemaphoreType.DMA((LEVELS + 1,))],
        compiler_params=limit(2),
        name="fetch",
    )(near(after), far(phases))


def box_sums_kernel(counts_ref, after_ref, tag_hbm_ref, rows_ref, keep_ref, send_ref, tag_ref, held, sems):
    step = WIDTH // FETCHES
    tags = pltpu.make_async_copy(tag_hbm_ref, tag_ref, sems.at[FETCHES])
    tags.start()
    copies = []
    for i in range(FETCHES):
        some = pl.ds(i * step, step)
        copies.append(pltpu.make_async_copy(rows_ref.at[some], held.at[some], sems.at[i]))
        copies[-1].start()
    tags.wait()
    slot = lax.broadcasted_iota(jnp.int32, (BOXES, WIDTH), 1)
    label = lax.broadcasted_iota(jnp.int32, (BOXES, WIDTH), 0)
    first = place_of("core") == 0

    def picks(j):
        hit = jnp.logical_and(tag_ref[j : j + 1, :] == label, slot < counts_ref[0, j])
        return jnp.where(hit, 1.0, 0.0).astype(jnp.bfloat16)

    for i in range(FETCHES):
        copies[i].wait()
        for j in range(i * step, (i + 1) * step, 2):
            left = jnp.concatenate([picks(j), picks(j + 1)], axis=0)
            right = jnp.concatenate([held[j], held[j + 1]], axis=1)
            sums = jnp.dot(left, right, preferred_element_type=jnp.float32)
            even, odd = sums[:BOXES, :WIDTH], sums[BOXES:, WIDTH:]
            keep_ref[j // 2] = jnp.where(first, even, odd).astype(jnp.bfloat16)
            send_ref[j // 2] = jnp.where(first, odd, even).astype(jnp.bfloat16)


def box_sums(counts, after, tag, rows):
    owners = rows.shape[0]
    return kernel_call(
        box_sums_kernel,
        in_specs=[SMEM, ANY, ANY, ANY],
        out_specs=[VMEM] * 2,
        out_shape=[pltpu.VMEM((owners // 2, BOXES, WIDTH), jnp.bfloat16)] * 2,
        scratch_shapes=[
            pltpu.VMEM(tag.shape, jnp.int32),
            pltpu.VMEM(rows.shape, jnp.bfloat16),
            pltpu.SemaphoreType.DMA((FETCHES + 1,)),
        ],
        compiler_params=limit(8),
        name="box_sums",
    )(counts, near(after), far(tag), far(rows))


def spread_kernel(part, inner, after_ref, *refs):
    parts, outs = refs[:-ALONG], refs[-ALONG:]
    place = place_of(part)
    for k, out_ref in enumerate(outs):
        there = jnp.bitwise_xor(place, k)
        if inner:
            for i in range(out_ref.shape[0]):
                total = sum(p[i * ALONG + there].astype(jnp.float32) for p in parts)
                out_ref[i] = total.astype(out_ref.dtype)
        else:
            some = pl.ds(there * out_ref.shape[0], out_ref.shape[0])
            out_ref[...] = sum(p[some].astype(jnp.float32) for p in parts).astype(out_ref.dtype)


def spread(part, inner, after, parts, sent):
    owners = parts[0].shape[0] // ALONG
    kinds = [jnp.float32] + [sent] * (ALONG - 1)
    return kernel_call(
        functools.partial(spread_kernel, part, inner),
        in_specs=[ANY] + [VMEM] * len(parts),
        out_specs=[VMEM] * ALONG,
        out_shape=[pltpu.VMEM((owners, BOXES, WIDTH), kind) for kind in kinds],
        compiler_params=limit(4),
        name="by_" + part,
    )(near(after), *map(near, parts))


def add_kernel(after_ref, *refs):
    refs[-1][...] = sum(r[...] for r in refs[:-1])


def add(after, parts):
    return kernel_call(
        add_kernel,
        in_specs=[ANY] + [VMEM] * len(parts),
        out_specs=VMEM,
        out_shape=pltpu.VMEM(parts[0].shape, jnp.float32),
        compiler_params=limit(4),
        name="add",
    )(near(after), *map(near, parts))


def expand_kernel(map_ref, *refs):
    parts, (mine_ref, other_ref) = refs[:-2], refs[-2:]
    place = place_of("x")
    for there, out_ref in ((place, mine_ref), (jnp.bitwise_xor(place, 1), other_ref)):
        total = sum(p[there] for p in parts).astype(jnp.bfloat16)
        out_ref[...] = jnp.dot(total, map_ref[...], preferred_element_type=jnp.float32)


def expand(source_map, parts):
    return kernel_call(
        expand_kernel,
        in_specs=[VMEM] * (1 + len(parts)),
        out_specs=[VMEM] * 2,
        out_shape=[pltpu.VMEM((BOXES, WIDTH), jnp.float32)] * 2,
        compiler_params=limit(4),
        name="expand",
    )(near(source_map), *map(near, parts))


def mats_kernel(after_ref, trans_ref, *out_refs):
    for level, out_ref in enumerate(out_refs):
        place = place_of(("x", "core", "x", "z")[level])
        pair = trans_ref[level, lax.rem(lax.div(place, jnp.int32(1 + (level == 2))), jnp.int32(2))]
        out_ref[:, :WIDTH] = pair[0].T
        out_ref[:, WIDTH:] = pair[1].T


def pick_mats(after, trans):
    return kernel_call(
        mats_kernel,
        in_specs=[ANY, VMEM],
        out_specs=[VMEM] * LEVELS,
        out_shape=[pltpu.VMEM((WIDTH, 2 * WIDTH), jnp.bfloat16)] * LEVELS,
        compiler_params=limit(4),
        name="mats",
    )(near(after), near(trans))


def column(x_ref, box):
    row = jnp.broadcast_to(x_ref[box : box + 1, :], (8, WIDTH))
    return row.T[:, :1]


def first_kernel(start, boxes, skip, x_ref, other_x_ref, mats_ref, phases_ref, other_ref, *rest):
    out_ref = rest[-1]
    per = min(boxes, SPAN // DIRS)
    for b in range(0, boxes, per):
        both = []
        for box in range(start + b, start + b + per):
            cols = pl.ds(box * DIRS, DIRS)
            mine = column(x_ref, box)
            state = turn(mine[:HALF], mine[HALF:], *cos_sin(phases_ref[0, :, cols]))
            theirs = column(other_x_ref, box)
            there = pl.ds((box - skip) * DIRS, DIRS)
            angle = other_ref[:, there].astype(jnp.int32).astype(jnp.float32) * (1.0 / TURN)
            partner = turn(theirs[:HALF], theirs[HALF:], *cos_sin(angle))
            both.append(jnp.concatenate([state, partner], axis=0))
        mixed = jnp.dot(mats_ref[...], jnp.concatenate(both, axis=1), preferred_element_type=jnp.float32)
        cols = pl.ds((start + b) * DIRS, per * DIRS)
        out_ref[:, b * DIRS : (b + per) * DIRS] = turn(mixed[:HALF], mixed[HALF:], *cos_sin(phases_ref[1, :, cols]))


def first_level(start, boxes, x, other_x, mats, phases, others, after):
    piece = 0
    while start >= sum(SENDS[: piece + 1]):
        piece += 1
    return kernel_call(
        functools.partial(first_kernel, start, boxes, sum(SENDS[:piece])),
        in_specs=[VMEM] * 5 + [ANY] * len(after),
        out_specs=VMEM,
        out_shape=pltpu.VMEM((WIDTH, boxes * DIRS), jnp.bfloat16),
        compiler_params=limit(8),
        name="first_level",
    )(near(x), near(other_x), near(mats), near(phases), near(others[piece]), *map(near, after))


def mix(start, level, cols, state_ref, partner_ref, mats_ref, phases_ref):
    both = jnp.concatenate([state_ref[:, cols], partner_ref[:, cols]], axis=0)
    mixed = jnp.dot(mats_ref[...], both, preferred_element_type=jnp.float32)
    there = pl.ds(start * DIRS + cols.start, cols.size)
    return turn(mixed[:HALF], mixed[HALF:], *cos_sin(phases_ref[level + 1, :, there]))


def spans(boxes):
    size = min(boxes * DIRS, SPAN)
    return [pl.ds(b, size) for b in range(0, boxes * DIRS, size)]


def level_kernel(start, boxes, level, state_ref, partner_ref, mats_ref, phases_ref, *rest):
    out_ref = rest[-1]
    for cols in spans(boxes):
        out_ref[:, cols] = mix(start, level, cols, state_ref, partner_ref, mats_ref, phases_ref)


def next_level(start, boxes, level, state, partner, mats, phases, after):
    return kernel_call(
        functools.partial(level_kernel, start, boxes, level),
        in_specs=[VMEM] * 4 + [ANY] * len(after),
        out_specs=VMEM,
        out_shape=pltpu.VMEM((WIDTH, boxes * DIRS), jnp.bfloat16),
        compiler_params=limit(8),
        name="level_%d" % level,
    )(near(state), near(partner), near(mats), near(phases), *map(near, after))


def last_kernel(start, boxes, state_ref, partner_ref, mats_ref, phases_ref, *rest):
    out_ref, token_ref, held, sems = rest[-4:]
    token_ref[...] = jnp.zeros_like(token_ref)
    copies = []
    for i, cols in enumerate(spans(boxes)):
        held[:, cols] = mix(start, LEVELS - 1, cols, state_ref, partner_ref, mats_ref, phases_ref)
        there = pl.ds(start * DIRS + cols.start, cols.size)
        copies.append(pltpu.make_async_copy(held.at[:, cols], out_ref.at[:, there], sems.at[i]))
        copies[-1].start()
    for copy in copies:
        copy.wait()


def last_level(start, boxes, state, partner, mats, phases, before, after):
    kept = [] if before is None else [far(before)]

    return kernel_call(
        functools.partial(last_kernel, start, boxes),
        in_specs=[VMEM] * 4 + [ANY] * (len(kept) + len(after)),
        out_specs=[ANY, VMEM],
        out_shape=[jax.ShapeDtypeStruct((WIDTH, ROWS), jnp.bfloat16), pltpu.VMEM((8, WIDTH), jnp.float32)],
        input_output_aliases={4: 0} if kept else {},
        scratch_shapes=[
            pltpu.VMEM((WIDTH, boxes * DIRS), jnp.bfloat16),
            pltpu.SemaphoreType.DMA((len(spans(boxes)),)),
        ],
        compiler_params=limit(8),
        name="last_level",
    )(near(state), near(partner), near(mats), near(phases), *kept, *map(near, after))


def move(value, axis, mask):
    return lax.ppermute(value, axis, [(s, s ^ mask) for s in range(lax.axis_size(axis))])


def per_device(currents, counts, box_of, source_map, phases, trans):
    turns = encode(phases)
    others = [move(t, "bx", 1) for t in turns]
    keep, send = box_sums(counts, turns[0], box_of[0], currents[0])
    got = move(send, "by", 1)
    own, *sent = spread("z", True, keep, [keep, got], jnp.bfloat16)
    angles = fetch(own, phases)
    got = [move(v, "by", 2 * k + 2) for k, v in enumerate(sent)]
    own, *sent = spread("y", False, angles, [own] + got, jnp.float32)
    mats = pick_mats(own, trans)
    row = add(mats[0], [own] + [move(v, "bx", 4 * k + 4) for k, v in enumerate(sent)])
    mine, theirs = expand(source_map, [row] + [move(row, "bx", k) for k in (1, 2, 3)])

    starts = [sum(PARTS[:i]) for i in range(len(PARTS))]
    count = len(PARTS)
    states = [{}, {}, {}, {}]
    latest = []

    def step(level, i):
        if not 0 <= i < count:
            return
        where = (starts[i], PARTS[i])
        after = latest[-1:]
        if level == 0:
            done = first_level(*where, mine, theirs, mats[0], angles, others, after)
        else:
            value = states[level - 1][i]
            other = move(value, *(("by", 1), ("bx", 2), ("by", 2))[level - 1])
            if level < 3:
                done = next_level(*where, level, value, other, mats[level], angles, after)
            else:
                states[3][i], done = last_level(*where, value, other, mats[level], angles, states[3].get(i - 1), after)
        if level < 3:
            states[level][i] = done
        latest.append(done)

    for i in range(-AHEAD, count + 2):
        step(0, i + AHEAD)
        step(1, i + AHEAD - 1)
        step(2, i)
        step(3, i - 2)
    return states[3][count - 1]


def solution(mesh):
    placed = (
        P(("bx", "by"), None, None, None),
        P(("bx", "by"), None),
        P(("bx", "by"), None, None),
        P(),
        P(None, None, ("bx", "by")),
        P(),
    )
    return jax.shard_map(
        per_device, mesh=mesh, in_specs=placed, out_specs=P(None, ("bx", "by")), check_vma=False
    )
```

```python
import functools

import jax
import jax.numpy as jnp
from jax import lax
from jax.experimental import pallas as pl
from jax.experimental.pallas import tpu as pltpu
from jax.sharding import PartitionSpec as P

BOXES = 16
DIRS = 512
HALF = 64
WIDTH = 128
ROWS = BOXES * DIRS
LEVELS = 4
PARTS = (2, 2, 2, 2, 2, 2, 2, 2)
GROUPS = (1, 1, 2, 2, 2)
ORDER = "a0 a1 b0 a2 b1 b2 c0 a3 b3 c1 b4 c2 d0 a4 b5 c3 d1 b6 c4 d2 b7 c5 d3 c6 d4 c7 d5 d6 d7"
SPAN = 1024
FETCHES = 4
ALONG = 4
FLOPS = 10**10
MIB = 1 << 20

TURN = 32767.0 / 3.141592653589793
SIN_HALF = (0.7071043848991394, -0.02945953793823719, 0.0003670926089398563, -2.0290131033107173e-06)
COS_HALF = (
    1.4142135381698608,
    -0.17677636444568634,
    0.003682575887069106,
    -3.061274401261471e-05,
    1.2791403491974052e-07,
)

ANY = pl.BlockSpec(memory_space=pl.ANY)
VMEM = pl.BlockSpec(memory_space=pltpu.VMEM)
SMEM = pl.BlockSpec(memory_space=pltpu.SMEM)


def near(value):
    return pltpu.with_memory_space_constraint(value, pltpu.VMEM)


def far(value):
    return pltpu.with_memory_space_constraint(value, pltpu.HBM)


def limit(mib):
    return pltpu.CompilerParams(vmem_limit_bytes=mib * MIB)


def kernel_call(*args, flops=1000, **kwargs):
    cost = pl.CostEstimate(flops=flops, bytes_accessed=1000, transcendentals=0)
    return pl.pallas_call(*args, cost_estimate=cost, **kwargs)


def place_of(part):
    axis, shift, count = {"core": ("by", 0, 2), "z": ("by", 1, 4), "x": ("bx", 0, 4), "y": ("bx", 2, 4)}[part]
    return lax.rem(lax.div(lax.axis_index(axis).astype(jnp.int32), jnp.int32(1 << shift)), jnp.int32(count))


def horner(terms, square):
    total = jnp.full_like(square, terms[-1])
    for term in terms[-2::-1]:
        total = total * square + term
    return total


def cos_sin(angle):
    square = angle * angle
    sine = horner(SIN_HALF, square) * angle
    cosine = horner(COS_HALF, square)
    return 1.0 - sine * sine, sine * cosine


def turn(re, im, cosine, sine):
    top = re * cosine - im * sine
    low = re * sine + im * cosine
    return jnp.concatenate([top, low], axis=0).astype(jnp.bfloat16)


def encode_kernel(phases_ref, out_ref, held, sems):
    span = ROWS // FETCHES
    copies = []
    for i in range(FETCHES):
        cols = pl.ds(i * span, span)
        copies.append(pltpu.make_async_copy(phases_ref.at[0, :, cols], held.at[:, cols], sems.at[i]))
        copies[-1].start()
    for i in range(FETCHES):
        copies[i].wait()
        cols = pl.ds(i * span, span)
        out_ref[:, cols] = jnp.round(held[:, cols] * TURN).astype(jnp.int32).astype(jnp.int16)


def encode(phases):
    return kernel_call(
        encode_kernel,
        in_specs=[ANY],
        out_specs=VMEM,
        out_shape=pltpu.VMEM((HALF, ROWS), jnp.int16),
        scratch_shapes=[pltpu.VMEM((HALF, ROWS), jnp.float32), pltpu.SemaphoreType.DMA((FETCHES,))],
        compiler_params=limit(8),
        name="encode",
    )(far(phases))


def fetch_kernel(first, after_ref, phases_ref, out_ref, sems):
    copies = []
    for k in range(out_ref.shape[0]):
        copies.append(pltpu.make_async_copy(phases_ref.at[first + k], out_ref.at[k], sems.at[k]))
        copies[-1].start()
    for copy in copies:
        copy.wait()


def fetch(first, count, after, phases):
    return kernel_call(
        functools.partial(fetch_kernel, first),
        in_specs=[ANY, ANY],
        out_specs=VMEM,
        out_shape=pltpu.VMEM((count, HALF, ROWS), jnp.float32),
        scratch_shapes=[pltpu.SemaphoreType.DMA((count,))],
        compiler_params=limit(2),
        name="fetch",
    )(near(after), far(phases))


def box_sums_kernel(counts_ref, after_ref, tag_hbm_ref, rows_ref, keep_ref, send_ref, tag_ref, held, sems):
    step = WIDTH // FETCHES
    tags = pltpu.make_async_copy(tag_hbm_ref, tag_ref, sems.at[FETCHES])
    tags.start()
    copies = []
    for i in range(FETCHES):
        some = pl.ds(i * step, step)
        copies.append(pltpu.make_async_copy(rows_ref.at[some], held.at[some], sems.at[i]))
        copies[-1].start()
    tags.wait()
    slot = lax.broadcasted_iota(jnp.int32, (BOXES, WIDTH), 1)
    label = lax.broadcasted_iota(jnp.int32, (BOXES, WIDTH), 0)
    first = place_of("core") == 0

    def picks(j):
        hit = jnp.logical_and(tag_ref[j : j + 1, :] == label, slot < counts_ref[0, j])
        return jnp.where(hit, 1.0, 0.0).astype(jnp.bfloat16)

    for i in range(FETCHES):
        copies[i].wait()
        for j in range(i * step, (i + 1) * step, 2):
            left = jnp.concatenate([picks(j), picks(j + 1)], axis=0)
            right = jnp.concatenate([held[j], held[j + 1]], axis=1)
            sums = jnp.dot(left, right, preferred_element_type=jnp.float32)
            even, odd = sums[:BOXES, :WIDTH], sums[BOXES:, WIDTH:]
            keep_ref[j // 2] = jnp.where(first, even, odd).astype(jnp.bfloat16)
            send_ref[j // 2] = jnp.where(first, odd, even).astype(jnp.bfloat16)


def box_sums(counts, after, tag, rows):
    owners = rows.shape[0]
    return kernel_call(
        box_sums_kernel,
        in_specs=[SMEM, ANY, ANY, ANY],
        out_specs=[VMEM] * 2,
        out_shape=[pltpu.VMEM((owners // 2, BOXES, WIDTH), jnp.bfloat16)] * 2,
        scratch_shapes=[
            pltpu.VMEM(tag.shape, jnp.int32),
            pltpu.VMEM(rows.shape, jnp.bfloat16),
            pltpu.SemaphoreType.DMA((FETCHES + 1,)),
        ],
        compiler_params=limit(8),
        name="box_sums",
    )(counts, near(after), far(tag), far(rows))


def spread_kernel(part, inner, after_ref, *refs):
    parts, outs = refs[:-ALONG], refs[-ALONG:]
    place = place_of(part)
    for k, out_ref in enumerate(outs):
        there = jnp.bitwise_xor(place, k)
        if inner:
            for i in range(out_ref.shape[0]):
                total = sum(p[i * ALONG + there].astype(jnp.float32) for p in parts)
                out_ref[i] = total.astype(out_ref.dtype)
        else:
            some = pl.ds(there * out_ref.shape[0], out_ref.shape[0])
            out_ref[...] = sum(p[some].astype(jnp.float32) for p in parts).astype(out_ref.dtype)


def spread(part, inner, after, parts, sent):
    owners = parts[0].shape[0] // ALONG
    kinds = [jnp.float32] + [sent] * (ALONG - 1)
    return kernel_call(
        functools.partial(spread_kernel, part, inner),
        in_specs=[ANY] + [VMEM] * len(parts),
        out_specs=[VMEM] * ALONG,
        out_shape=[pltpu.VMEM((owners, BOXES, WIDTH), kind) for kind in kinds],
        compiler_params=limit(4),
        name="by_" + part,
    )(near(after), *map(near, parts))


def add_kernel(after_ref, *refs):
    refs[-1][...] = sum(r[...] for r in refs[:-1])


def add(after, parts):
    return kernel_call(
        add_kernel,
        in_specs=[ANY] + [VMEM] * len(parts),
        out_specs=VMEM,
        out_shape=pltpu.VMEM(parts[0].shape, jnp.float32),
        compiler_params=limit(4),
        name="add",
    )(near(after), *map(near, parts))


def expand_kernel(after_ref, map_ref, *refs):
    parts, (mine_ref, other_ref) = refs[:-2], refs[-2:]
    place = place_of("x")
    for there, out_ref in ((place, mine_ref), (jnp.bitwise_xor(place, 1), other_ref)):
        total = sum(p[there] for p in parts).astype(jnp.bfloat16)
        out_ref[...] = jnp.dot(total, map_ref[...], preferred_element_type=jnp.float32)


def expand(after, source_map, parts):
    return kernel_call(
        expand_kernel,
        in_specs=[ANY] + [VMEM] * (1 + len(parts)),
        out_specs=[VMEM] * 2,
        out_shape=[pltpu.VMEM((BOXES, WIDTH), jnp.float32)] * 2,
        compiler_params=limit(4),
        name="expand",
    )(near(after), near(source_map), *map(near, parts))


def mats_kernel(after_ref, trans_ref, *out_refs):
    for level, out_ref in enumerate(out_refs):
        place = place_of(("x", "core", "x", "z")[level])
        pair = trans_ref[level, lax.rem(lax.div(place, jnp.int32(1 + (level == 2))), jnp.int32(2))]
        out_ref[:, :WIDTH] = pair[0].T
        out_ref[:, WIDTH:] = pair[1].T


def pick_mats(after, trans):
    return kernel_call(
        mats_kernel,
        in_specs=[ANY, VMEM],
        out_specs=[VMEM] * LEVELS,
        out_shape=[pltpu.VMEM((WIDTH, 2 * WIDTH), jnp.bfloat16)] * LEVELS,
        compiler_params=limit(4),
        name="mats",
    )(near(after), near(trans))


def column(x_ref, box):
    row = jnp.broadcast_to(x_ref[box : box + 1, :], (8, WIDTH))
    return row.T[:, :1]


def first_kernel(start, boxes, x_ref, other_x_ref, mats_ref, phases_ref, other_ref, *rest):
    out_ref = rest[-1]
    per = min(boxes, SPAN // DIRS)
    for b in range(0, boxes, per):
        both = []
        for box in range(start + b, start + b + per):
            cols = pl.ds(box * DIRS, DIRS)
            mine = column(x_ref, box)
            state = turn(mine[:HALF], mine[HALF:], *cos_sin(phases_ref[0, :, cols]))
            theirs = column(other_x_ref, box)
            angle = other_ref[:, cols].astype(jnp.int32).astype(jnp.float32) * (1.0 / TURN)
            partner = turn(theirs[:HALF], theirs[HALF:], *cos_sin(angle))
            both.append(jnp.concatenate([state, partner], axis=0))
        mixed = jnp.dot(mats_ref[...], jnp.concatenate(both, axis=1), preferred_element_type=jnp.float32)
        cols = pl.ds((start + b) * DIRS, per * DIRS)
        out_ref[:, b * DIRS : (b + per) * DIRS] = turn(mixed[:HALF], mixed[HALF:], *cos_sin(phases_ref[1, :, cols]))


def first_level(start, boxes, x, other_x, mats, phases, others, after):
    return kernel_call(
        functools.partial(first_kernel, start, boxes),
        in_specs=[VMEM] * 5 + [ANY] * len(after),
        out_specs=VMEM,
        out_shape=pltpu.VMEM((WIDTH, boxes * DIRS), jnp.bfloat16),
        compiler_params=limit(8),
        flops=FLOPS,
        name="a_%d" % start,
    )(near(x), near(other_x), near(mats), near(phases), near(others), *map(near, after))


def mix(start, skip, slot, cols, state_ref, partner_ref, mats_ref, phases_ref):
    here = pl.ds((start - skip) * DIRS + cols.start, cols.size)
    there = pl.ds(start * DIRS + cols.start, cols.size)
    both = jnp.concatenate([state_ref[:, here], partner_ref[:, here]], axis=0)
    mixed = jnp.dot(mats_ref[...], both, preferred_element_type=jnp.float32)
    return turn(mixed[:HALF], mixed[HALF:], *cos_sin(phases_ref[slot, :, there]))


def spans(boxes):
    size = min(boxes * DIRS, SPAN)
    return [pl.ds(b, size) for b in range(0, boxes * DIRS, size)]


def level_kernel(start, boxes, skip, slot, state_ref, partner_ref, mats_ref, phases_ref, *rest):
    out_ref = rest[-1]
    for cols in spans(boxes):
        out_ref[:, cols] = mix(start, skip, slot, cols, state_ref, partner_ref, mats_ref, phases_ref)


def next_level(name, start, boxes, skip, slot, state, partner, mats, phases, after):
    return kernel_call(
        functools.partial(level_kernel, start, boxes, skip, slot),
        in_specs=[VMEM] * 4 + [ANY] * len(after),
        out_specs=VMEM,
        out_shape=pltpu.VMEM((WIDTH, boxes * DIRS), jnp.bfloat16),
        compiler_params=limit(8),
        flops=FLOPS,
        name="%s_%d" % (name, start),
    )(near(state), near(partner), near(mats), near(phases), *map(near, after))


def flush_kernel(*refs):
    parts, out_ref, sems = refs[:-2], refs[-2], refs[-1]
    copies, at = [], 0
    for i, part in enumerate(parts):
        size = part.shape[1]
        copies.append(pltpu.make_async_copy(part, out_ref.at[:, pl.ds(at, size)], sems.at[i]))
        copies[-1].start()
        at += size
    for copy in copies:
        copy.wait()


def flush(parts):
    return kernel_call(
        flush_kernel,
        in_specs=[VMEM] * len(parts),
        out_specs=ANY,
        out_shape=jax.ShapeDtypeStruct((WIDTH, ROWS), jnp.bfloat16),
        scratch_shapes=[pltpu.SemaphoreType.DMA((len(parts),))],
        compiler_params=limit(2),
        flops=FLOPS,
        name="flush",
    )(*map(near, parts))


def last_kernel(start, boxes, slot, state_ref, partner_ref, mats_ref, phases_ref, before_ref, out_ref, held, sems):
    copies = []
    for i, cols in enumerate(spans(boxes)):
        held[:, cols] = mix(start, start, slot, cols, state_ref, partner_ref, mats_ref, phases_ref)
        there = pl.ds(start * DIRS + cols.start, cols.size)
        copies.append(pltpu.make_async_copy(held.at[:, cols], out_ref.at[:, there], sems.at[i]))
        copies[-1].start()
    for copy in copies:
        copy.wait()


def last_level(start, boxes, slot, state, partner, mats, phases, before):
    return kernel_call(
        functools.partial(last_kernel, start, boxes, slot),
        in_specs=[VMEM] * 4 + [ANY],
        out_specs=ANY,
        out_shape=jax.ShapeDtypeStruct((WIDTH, ROWS), jnp.bfloat16),
        input_output_aliases={4: 0},
        scratch_shapes=[
            pltpu.VMEM((WIDTH, boxes * DIRS), jnp.bfloat16),
            pltpu.SemaphoreType.DMA((len(spans(boxes)),)),
        ],
        compiler_params=limit(8),
        flops=FLOPS,
        name="last",
    )(near(state), near(partner), near(mats), near(phases), far(before))


def move(value, axis, mask):
    return lax.ppermute(value, axis, [(s, s ^ mask) for s in range(lax.axis_size(axis))])


def per_device(currents, counts, box_of, source_map, phases, trans):
    turns = encode(phases)
    others = move(turns, "bx", 1)
    keep, send = box_sums(counts, turns, box_of[0], currents[0])
    got = move(send, "by", 1)
    own, *sent = spread("z", True, keep, [keep, got], jnp.bfloat16)
    early = fetch(0, 2, own, phases)
    got = [move(v, "by", 2 * k + 2) for k, v in enumerate(sent)]
    own, *sent = spread("y", False, early, [own] + got, jnp.float32)
    mats = pick_mats(own, trans)
    row = add(mats[0], [own] + [move(v, "bx", 4 * k + 4) for k, v in enumerate(sent)])
    late = fetch(2, 3, row, phases)
    mine, theirs = expand(late, source_map, [row] + [move(row, "bx", k) for k in (1, 2, 3)])

    starts = [sum(PARTS[:i]) for i in range(len(PARTS))]
    groups = [range(sum(GROUPS[:g]), sum(GROUPS[: g + 1])) for g in range(len(GROUPS))]
    final = len(PARTS) - 1
    firsts, states, partners, out = {}, {}, {}, None
    after = []
    for name in ORDER.split():
        level, i = name[0], int(name[1:])
        if level == "a":
            start, boxes = starts[groups[i][0]], sum(PARTS[p] for p in groups[i])
            done = first_level(start, boxes, mine, theirs, mats[0], early, others, after)
            swapped = move(done, "by", 1)
            for p in groups[i]:
                firsts[p] = (start, done, swapped)
        elif level == "b":
            skip, value, other = firsts[i]
            done = next_level(level, starts[i], PARTS[i], skip, 0, value, other, mats[1], late, after)
            states[i], partners[i] = done, move(done, "bx", 2)
        elif level == "c":
            ends = (starts[i], PARTS[i], starts[i], 1)
            done = next_level(level, *ends, states[i], partners[i], mats[2], late, after)
            states[i], partners[i] = done, move(done, "by", 2)
        elif i < final:
            ends = (starts[i], PARTS[i], starts[i], 2)
            done = next_level(level, *ends, states[i], partners[i], mats[3], late, after)
            states[i] = done
        else:
            out = flush([states[p] for p in range(final)])
            return last_level(starts[i], PARTS[i], 2, states[i], partners[i], mats[3], late, out)
        after = [done]


def solution(mesh):
    placed = (
        P(("bx", "by"), None, None, None),
        P(("bx", "by"), None),
        P(("bx", "by"), None, None),
        P(),
        P(None, None, ("bx", "by")),
        P(),
    )
    return jax.shard_map(
        per_device, mesh=mesh, in_specs=placed, out_specs=P(None, ("bx", "by")), check_vma=False
    )
```

```python
import functools

import jax
import jax.numpy as jnp
from jax import lax
from jax.experimental import pallas as pl
from jax.experimental.pallas import tpu as pltpu
from jax.sharding import PartitionSpec as P

BOXES = 16
DIRS = 512
HALF = 64
WIDTH = 128
ROWS = BOXES * DIRS
LEVELS = 4
PARTS = (2, 2, 2, 2, 2, 2, 2, 2)
GROUPS = (1, 1, 2, 2, 2)
ORDER = "a0 a1 b0 a2 b1 b2 f c0 a3 b3 c1 b4 c2 d0 a4 b5 c3 d1 b6 c4 d2 b7 c5 d3 c6 d4 c7 d5 d6 d7"
SPAN = 1024
FETCHES = 4
ALONG = 4
FLOPS = 10**10
MIB = 1 << 20

TURN = 32767.0 / 3.141592653589793
SIN_HALF = (0.7071043848991394, -0.02945953793823719, 0.0003670926089398563, -2.0290131033107173e-06)
COS_HALF = (
    1.4142135381698608,
    -0.17677636444568634,
    0.003682575887069106,
    -3.061274401261471e-05,
    1.2791403491974052e-07,
)

ANY = pl.BlockSpec(memory_space=pl.ANY)
VMEM = pl.BlockSpec(memory_space=pltpu.VMEM)
SMEM = pl.BlockSpec(memory_space=pltpu.SMEM)


def near(value):
    return pltpu.with_memory_space_constraint(value, pltpu.VMEM)


def far(value):
    return pltpu.with_memory_space_constraint(value, pltpu.HBM)


def limit(mib):
    return pltpu.CompilerParams(vmem_limit_bytes=mib * MIB)


def kernel_call(*args, flops=1000, **kwargs):
    cost = pl.CostEstimate(flops=flops, bytes_accessed=1000, transcendentals=0)
    return pl.pallas_call(*args, cost_estimate=cost, **kwargs)


def place_of(part):
    axis, shift, count = {"core": ("by", 0, 2), "z": ("by", 1, 4), "x": ("bx", 0, 4), "y": ("bx", 2, 4)}[part]
    return lax.rem(lax.div(lax.axis_index(axis).astype(jnp.int32), jnp.int32(1 << shift)), jnp.int32(count))


def horner(terms, square):
    total = jnp.full_like(square, terms[-1])
    for term in terms[-2::-1]:
        total = total * square + term
    return total


def cos_sin(angle):
    square = angle * angle
    sine = horner(SIN_HALF, square) * angle
    cosine = horner(COS_HALF, square)
    return 1.0 - sine * sine, sine * cosine


def turn(re, im, cosine, sine):
    top = re * cosine - im * sine
    low = re * sine + im * cosine
    return jnp.concatenate([top, low], axis=0).astype(jnp.bfloat16)


def encode_kernel(phases_ref, out_ref, held, sems):
    span = ROWS // FETCHES
    copies = []
    for i in range(FETCHES):
        cols = pl.ds(i * span, span)
        copies.append(pltpu.make_async_copy(phases_ref.at[0, :, cols], held.at[:, cols], sems.at[i]))
        copies[-1].start()
    for i in range(FETCHES):
        copies[i].wait()
        cols = pl.ds(i * span, span)
        out_ref[:, cols] = jnp.round(held[:, cols] * TURN).astype(jnp.int32).astype(jnp.int16)


def encode(phases):
    return kernel_call(
        encode_kernel,
        in_specs=[ANY],
        out_specs=VMEM,
        out_shape=pltpu.VMEM((HALF, ROWS), jnp.int16),
        scratch_shapes=[pltpu.VMEM((HALF, ROWS), jnp.float32), pltpu.SemaphoreType.DMA((FETCHES,))],
        compiler_params=limit(8),
        name="encode",
    )(far(phases))


def fetch_kernel(first, after_ref, phases_ref, out_ref, sems):
    copies = []
    for k in range(out_ref.shape[0]):
        copies.append(pltpu.make_async_copy(phases_ref.at[first + k], out_ref.at[k], sems.at[k]))
        copies[-1].start()
    for copy in copies:
        copy.wait()


def fetch(first, count, after, phases):
    return kernel_call(
        functools.partial(fetch_kernel, first),
        in_specs=[ANY, ANY],
        out_specs=VMEM,
        out_shape=pltpu.VMEM((count, HALF, ROWS), jnp.float32),
        scratch_shapes=[pltpu.SemaphoreType.DMA((count,))],
        compiler_params=limit(2),
        name="fetch",
    )(near(after), far(phases))


def box_sums_kernel(counts_ref, after_ref, tag_hbm_ref, rows_ref, keep_ref, send_ref, tag_ref, held, sems):
    step = WIDTH // FETCHES
    tags = pltpu.make_async_copy(tag_hbm_ref, tag_ref, sems.at[FETCHES])
    tags.start()
    copies = []
    for i in range(FETCHES):
        some = pl.ds(i * step, step)
        copies.append(pltpu.make_async_copy(rows_ref.at[some], held.at[some], sems.at[i]))
        copies[-1].start()
    tags.wait()
    slot = lax.broadcasted_iota(jnp.int32, (BOXES, WIDTH), 1)
    label = lax.broadcasted_iota(jnp.int32, (BOXES, WIDTH), 0)
    first = place_of("core") == 0

    def picks(j):
        hit = jnp.logical_and(tag_ref[j : j + 1, :] == label, slot < counts_ref[0, j])
        return jnp.where(hit, 1.0, 0.0).astype(jnp.bfloat16)

    for i in range(FETCHES):
        copies[i].wait()
        for j in range(i * step, (i + 1) * step, 2):
            left = jnp.concatenate([picks(j), picks(j + 1)], axis=0)
            right = jnp.concatenate([held[j], held[j + 1]], axis=1)
            sums = jnp.dot(left, right, preferred_element_type=jnp.float32)
            even, odd = sums[:BOXES, :WIDTH], sums[BOXES:, WIDTH:]
            keep_ref[j // 2] = jnp.where(first, even, odd).astype(jnp.bfloat16)
            send_ref[j // 2] = jnp.where(first, odd, even).astype(jnp.bfloat16)


def box_sums(counts, after, tag, rows):
    owners = rows.shape[0]
    return kernel_call(
        box_sums_kernel,
        in_specs=[SMEM, ANY, ANY, ANY],
        out_specs=[VMEM] * 2,
        out_shape=[pltpu.VMEM((owners // 2, BOXES, WIDTH), jnp.bfloat16)] * 2,
        scratch_shapes=[
            pltpu.VMEM(tag.shape, jnp.int32),
            pltpu.VMEM(rows.shape, jnp.bfloat16),
            pltpu.SemaphoreType.DMA((FETCHES + 1,)),
        ],
        compiler_params=limit(8),
        name="box_sums",
    )(counts, near(after), far(tag), far(rows))


def deal_kernel(keep_ref, got_ref, out_ref):
    for y in range(ALONG):
        for x in range(ALONG):
            for z in range(ALONG):
                i = (y * ALONG + x) * ALONG + z
                total = keep_ref[i].astype(jnp.float32) + got_ref[i].astype(jnp.float32)
                out_ref[y * ALONG + z, x] = total.astype(jnp.bfloat16)


def deal(keep, got):
    return kernel_call(
        deal_kernel,
        in_specs=[VMEM] * 2,
        out_specs=VMEM,
        out_shape=pltpu.VMEM((ALONG * ALONG, ALONG, BOXES, WIDTH), jnp.bfloat16),
        compiler_params=limit(4),
        name="deal",
    )(near(keep), near(got))


def add_kernel(parts_ref, out_ref):
    out_ref[...] = sum(parts_ref[i].astype(jnp.float32) for i in range(parts_ref.shape[0]))


def add(parts):
    return kernel_call(
        add_kernel,
        in_specs=[VMEM],
        out_specs=VMEM,
        out_shape=pltpu.VMEM(parts.shape[1:], jnp.float32),
        compiler_params=limit(4),
        name="add",
    )(near(parts))


def expand_kernel(after_ref, map_ref, *refs):
    parts, (mine_ref, other_ref) = refs[:-2], refs[-2:]
    place = place_of("x")
    for there, out_ref in ((place, mine_ref), (jnp.bitwise_xor(place, 1), other_ref)):
        total = sum(p[there] for p in parts).astype(jnp.bfloat16)
        out_ref[...] = jnp.dot(total, map_ref[...], preferred_element_type=jnp.float32)


def expand(after, source_map, parts):
    return kernel_call(
        expand_kernel,
        in_specs=[ANY] + [VMEM] * (1 + len(parts)),
        out_specs=[VMEM] * 2,
        out_shape=[pltpu.VMEM((BOXES, WIDTH), jnp.float32)] * 2,
        compiler_params=limit(4),
        name="expand",
    )(near(after), near(source_map), *map(near, parts))


def mats_kernel(after_ref, trans_ref, *out_refs):
    for level, out_ref in enumerate(out_refs):
        place = place_of(("x", "core", "x", "z")[level])
        pair = trans_ref[level, lax.rem(lax.div(place, jnp.int32(1 + (level == 2))), jnp.int32(2))]
        out_ref[:, :WIDTH] = pair[0].T
        out_ref[:, WIDTH:] = pair[1].T


def pick_mats(after, trans):
    return kernel_call(
        mats_kernel,
        in_specs=[ANY, VMEM],
        out_specs=[VMEM] * LEVELS,
        out_shape=[pltpu.VMEM((WIDTH, 2 * WIDTH), jnp.bfloat16)] * LEVELS,
        compiler_params=limit(4),
        name="mats",
    )(near(after), near(trans))


def column(x_ref, box):
    row = jnp.broadcast_to(x_ref[box : box + 1, :], (8, WIDTH))
    return row.T[:, :1]


def first_kernel(start, boxes, x_ref, other_x_ref, mats_ref, phases_ref, other_ref, *rest):
    out_ref = rest[-1]
    per = min(boxes, SPAN // DIRS)
    for b in range(0, boxes, per):
        both = []
        for box in range(start + b, start + b + per):
            cols = pl.ds(box * DIRS, DIRS)
            mine = column(x_ref, box)
            state = turn(mine[:HALF], mine[HALF:], *cos_sin(phases_ref[0, :, cols]))
            theirs = column(other_x_ref, box)
            angle = other_ref[:, cols].astype(jnp.int32).astype(jnp.float32) * (1.0 / TURN)
            partner = turn(theirs[:HALF], theirs[HALF:], *cos_sin(angle))
            both.append(jnp.concatenate([state, partner], axis=0))
        mixed = jnp.dot(mats_ref[...], jnp.concatenate(both, axis=1), preferred_element_type=jnp.float32)
        cols = pl.ds((start + b) * DIRS, per * DIRS)
        out_ref[:, b * DIRS : (b + per) * DIRS] = turn(mixed[:HALF], mixed[HALF:], *cos_sin(phases_ref[1, :, cols]))


def first_level(start, boxes, x, other_x, mats, phases, others, after):
    return kernel_call(
        functools.partial(first_kernel, start, boxes),
        in_specs=[VMEM] * 5 + [ANY] * len(after),
        out_specs=VMEM,
        out_shape=pltpu.VMEM((WIDTH, boxes * DIRS), jnp.bfloat16),
        compiler_params=limit(8),
        flops=FLOPS,
        name="a_%d" % start,
    )(near(x), near(other_x), near(mats), near(phases), near(others), *map(near, after))


def mix(start, skip, slot, cols, state_ref, partner_ref, mats_ref, phases_ref):
    here = pl.ds((start - skip) * DIRS + cols.start, cols.size)
    there = pl.ds(start * DIRS + cols.start, cols.size)
    both = jnp.concatenate([state_ref[:, here], partner_ref[:, here]], axis=0)
    mixed = jnp.dot(mats_ref[...], both, preferred_element_type=jnp.float32)
    return turn(mixed[:HALF], mixed[HALF:], *cos_sin(phases_ref[slot, :, there]))


def spans(boxes):
    size = min(boxes * DIRS, SPAN)
    return [pl.ds(b, size) for b in range(0, boxes * DIRS, size)]


def level_kernel(start, boxes, skip, slot, state_ref, partner_ref, mats_ref, phases_ref, *rest):
    out_ref = rest[-1]
    for cols in spans(boxes):
        out_ref[:, cols] = mix(start, skip, slot, cols, state_ref, partner_ref, mats_ref, phases_ref)


def next_level(name, start, boxes, skip, slot, state, partner, mats, phases, after):
    return kernel_call(
        functools.partial(level_kernel, start, boxes, skip, slot),
        in_specs=[VMEM] * 4 + [ANY] * len(after),
        out_specs=VMEM,
        out_shape=pltpu.VMEM((WIDTH, boxes * DIRS), jnp.bfloat16),
        compiler_params=limit(8),
        flops=FLOPS,
        name="%s_%d" % (name, start),
    )(near(state), near(partner), near(mats), near(phases), *map(near, after))


def flush_kernel(*refs):
    parts, out_ref, sems = refs[:-2], refs[-2], refs[-1]
    copies, at = [], 0
    for i, part in enumerate(parts):
        size = part.shape[1]
        copies.append(pltpu.make_async_copy(part, out_ref.at[:, pl.ds(at, size)], sems.at[i]))
        copies[-1].start()
        at += size
    for copy in copies:
        copy.wait()


def flush(parts):
    return kernel_call(
        flush_kernel,
        in_specs=[VMEM] * len(parts),
        out_specs=ANY,
        out_shape=jax.ShapeDtypeStruct((WIDTH, ROWS), jnp.bfloat16),
        scratch_shapes=[pltpu.SemaphoreType.DMA((len(parts),))],
        compiler_params=limit(2),
        flops=FLOPS,
        name="flush",
    )(*map(near, parts))


def last_kernel(start, boxes, slot, state_ref, partner_ref, mats_ref, phases_ref, before_ref, out_ref, held, sems):
    copies = []
    for i, cols in enumerate(spans(boxes)):
        held[:, cols] = mix(start, start, slot, cols, state_ref, partner_ref, mats_ref, phases_ref)
        there = pl.ds(start * DIRS + cols.start, cols.size)
        copies.append(pltpu.make_async_copy(held.at[:, cols], out_ref.at[:, there], sems.at[i]))
        copies[-1].start()
    for copy in copies:
        copy.wait()


def last_level(start, boxes, slot, state, partner, mats, phases, before):
    return kernel_call(
        functools.partial(last_kernel, start, boxes, slot),
        in_specs=[VMEM] * 4 + [ANY],
        out_specs=ANY,
        out_shape=jax.ShapeDtypeStruct((WIDTH, ROWS), jnp.bfloat16),
        input_output_aliases={4: 0},
        scratch_shapes=[
            pltpu.VMEM((WIDTH, boxes * DIRS), jnp.bfloat16),
            pltpu.SemaphoreType.DMA((len(spans(boxes)),)),
        ],
        compiler_params=limit(8),
        flops=FLOPS,
        name="last",
    )(near(state), near(partner), near(mats), near(phases), far(before))


def move(value, axis, mask):
    return lax.ppermute(value, axis, [(s, s ^ mask) for s in range(lax.axis_size(axis))])


def per_device(currents, counts, box_of, source_map, phases, trans):
    turns = encode(phases)
    others = move(turns, "bx", 1)
    keep, send = box_sums(counts, turns, box_of[0], currents[0])
    got = move(send, "by", 1)
    plane = [
        [(y * ALONG + x) * 2 * ALONG + z * 2 + core for y in range(ALONG) for z in range(ALONG)]
        for x in range(ALONG)
        for core in range(2)
    ]
    parts = lax.all_to_all(
        deal(keep, got), ("bx", "by"), split_axis=0, concat_axis=0, tiled=True, axis_index_groups=plane
    )
    row = add(parts)
    early = fetch(0, 3, row, phases)
    mats = pick_mats(row, trans)
    mine, theirs = expand(early, source_map, [row] + [move(row, "bx", k) for k in (1, 2, 3)])

    starts = [sum(PARTS[:i]) for i in range(len(PARTS))]
    groups = [range(sum(GROUPS[:g]), sum(GROUPS[: g + 1])) for g in range(len(GROUPS))]
    final = len(PARTS) - 1
    firsts, states, partners, out = {}, {}, {}, None
    after = []
    for name in ORDER.split():
        if name == "f":
            after = [late := fetch(3, 2, after[0], phases)]
            continue
        level, i = name[0], int(name[1:])
        if level == "a":
            start, boxes = starts[groups[i][0]], sum(PARTS[p] for p in groups[i])
            done = first_level(start, boxes, mine, theirs, mats[0], early, others, after)
            swapped = move(done, "by", 1)
            for p in groups[i]:
                firsts[p] = (start, done, swapped)
        elif level == "b":
            skip, value, other = firsts[i]
            done = next_level(level, starts[i], PARTS[i], skip, 2, value, other, mats[1], early, after)
            states[i], partners[i] = done, move(done, "bx", 2)
        elif level == "c":
            ends = (starts[i], PARTS[i], starts[i], 0)
            done = next_level(level, *ends, states[i], partners[i], mats[2], late, after)
            states[i], partners[i] = done, move(done, "by", 2)
        elif i < final:
            ends = (starts[i], PARTS[i], starts[i], 1)
            done = next_level(level, *ends, states[i], partners[i], mats[3], late, after)
            states[i] = done
        else:
            out = flush([states[p] for p in range(final)])
            return last_level(starts[i], PARTS[i], 1, states[i], partners[i], mats[3], late, out)
        after = [done]


def solution(mesh):
    placed = (
        P(("bx", "by"), None, None, None),
        P(("bx", "by"), None),
        P(("bx", "by"), None, None),
        P(),
        P(None, None, ("bx", "by")),
        P(),
    )
    return jax.shard_map(
        per_device, mesh=mesh, in_specs=placed, out_specs=P(None, ("bx", "by")), check_vma=False
    )
```

```python
import functools

import jax
import jax.numpy as jnp
from jax import lax
from jax.experimental import pallas as pl
from jax.experimental.pallas import tpu as pltpu
from jax.sharding import PartitionSpec as P

BOXES = 16
DIRS = 512
HALF = 64
WIDTH = 128
ROWS = BOXES * DIRS
LEVELS = 4
PARTS = (2, 2, 2, 2, 2, 2, 2, 2)
GROUPS = (1, 1, 2, 2, 2)
ORDER = "a0 a1 b0 a2 b1 b2 f c0 a3 b3 c1 b4 c2 d0 a4 b5 c3 d1 b6 c4 d2 b7 c5 d3 c6 d4 c7 d5 d6 d7"
SPAN = 1024
FETCHES = 4
ALONG = 4
FLOPS = 10**10
MIB = 1 << 20

TURN = 32767.0 / 3.141592653589793
SIN_HALF = (0.7071043848991394, -0.02945953793823719, 0.0003670926089398563, -2.0290131033107173e-06)
COS_HALF = (
    1.4142135381698608,
    -0.17677636444568634,
    0.003682575887069106,
    -3.061274401261471e-05,
    1.2791403491974052e-07,
)

ANY = pl.BlockSpec(memory_space=pl.ANY)
VMEM = pl.BlockSpec(memory_space=pltpu.VMEM)
SMEM = pl.BlockSpec(memory_space=pltpu.SMEM)


def near(value):
    return pltpu.with_memory_space_constraint(value, pltpu.VMEM)


def far(value):
    return pltpu.with_memory_space_constraint(value, pltpu.HBM)


def limit(mib):
    return pltpu.CompilerParams(vmem_limit_bytes=mib * MIB)


def kernel_call(*args, flops=1000, **kwargs):
    cost = pl.CostEstimate(flops=flops, bytes_accessed=1000, transcendentals=0)
    return pl.pallas_call(*args, cost_estimate=cost, **kwargs)


def place_of(part):
    axis, shift, count = {"core": ("by", 0, 2), "z": ("by", 1, 4), "x": ("bx", 0, 4), "y": ("bx", 2, 4)}[part]
    return lax.rem(lax.div(lax.axis_index(axis).astype(jnp.int32), jnp.int32(1 << shift)), jnp.int32(count))


def horner(terms, square):
    total = jnp.full_like(square, terms[-1])
    for term in terms[-2::-1]:
        total = total * square + term
    return total


def cos_sin(angle):
    square = angle * angle
    sine = horner(SIN_HALF, square) * angle
    cosine = horner(COS_HALF, square)
    return 1.0 - sine * sine, sine * cosine


def turn(re, im, cosine, sine):
    top = re * cosine - im * sine
    low = re * sine + im * cosine
    return jnp.concatenate([top, low], axis=0).astype(jnp.bfloat16)


def encode_kernel(phases_ref, out_ref, held, sems):
    span = ROWS // FETCHES
    copies = []
    for i in range(FETCHES):
        cols = pl.ds(i * span, span)
        copies.append(pltpu.make_async_copy(phases_ref.at[0, :, cols], held.at[:, cols], sems.at[i]))
        copies[-1].start()
    for i in range(FETCHES):
        copies[i].wait()
        cols = pl.ds(i * span, span)
        out_ref[:, cols] = jnp.round(held[:, cols] * TURN).astype(jnp.int32).astype(jnp.int16)


def encode(phases):
    return kernel_call(
        encode_kernel,
        in_specs=[ANY],
        out_specs=VMEM,
        out_shape=pltpu.VMEM((HALF, ROWS), jnp.int16),
        scratch_shapes=[pltpu.VMEM((HALF, ROWS), jnp.float32), pltpu.SemaphoreType.DMA((FETCHES,))],
        compiler_params=limit(8),
        name="encode",
    )(far(phases))


def fetch_kernel(first, after_ref, phases_ref, out_ref, sems):
    copies = []
    for k in range(out_ref.shape[0]):
        copies.append(pltpu.make_async_copy(phases_ref.at[first + k], out_ref.at[k], sems.at[k]))
        copies[-1].start()
    for copy in copies:
        copy.wait()


def fetch(first, count, after, phases):
    return kernel_call(
        functools.partial(fetch_kernel, first),
        in_specs=[ANY, ANY],
        out_specs=VMEM,
        out_shape=pltpu.VMEM((count, HALF, ROWS), jnp.float32),
        scratch_shapes=[pltpu.SemaphoreType.DMA((count,))],
        compiler_params=limit(2),
        name="fetch",
    )(near(after), far(phases))


def box_sums_kernel(counts_ref, after_ref, tag_hbm_ref, rows_ref, keep_ref, send_ref, tag_ref, held, sems):
    step = WIDTH // FETCHES
    tags = pltpu.make_async_copy(tag_hbm_ref, tag_ref, sems.at[FETCHES])
    tags.start()
    copies = []
    for i in range(FETCHES):
        some = pl.ds(i * step, step)
        copies.append(pltpu.make_async_copy(rows_ref.at[some], held.at[some], sems.at[i]))
        copies[-1].start()
    tags.wait()
    slot = lax.broadcasted_iota(jnp.int32, (BOXES, WIDTH), 1)
    label = lax.broadcasted_iota(jnp.int32, (BOXES, WIDTH), 0)
    first = place_of("core") == 0

    def picks(j):
        hit = jnp.logical_and(tag_ref[j : j + 1, :] == label, slot < counts_ref[0, j])
        return jnp.where(hit, 1.0, 0.0).astype(jnp.bfloat16)

    for i in range(FETCHES):
        copies[i].wait()
        for j in range(i * step, (i + 1) * step, 2):
            left = jnp.concatenate([picks(j), picks(j + 1)], axis=0)
            right = jnp.concatenate([held[j], held[j + 1]], axis=1)
            sums = jnp.dot(left, right, preferred_element_type=jnp.float32)
            even, odd = sums[:BOXES, :WIDTH], sums[BOXES:, WIDTH:]
            keep_ref[j // 2] = jnp.where(first, even, odd).astype(jnp.bfloat16)
            send_ref[j // 2] = jnp.where(first, odd, even).astype(jnp.bfloat16)


def box_sums(counts, after, tag, rows):
    owners = rows.shape[0]
    return kernel_call(
        box_sums_kernel,
        in_specs=[SMEM, ANY, ANY, ANY],
        out_specs=[VMEM] * 2,
        out_shape=[pltpu.VMEM((owners // 2, BOXES, WIDTH), jnp.bfloat16)] * 2,
        scratch_shapes=[
            pltpu.VMEM(tag.shape, jnp.int32),
            pltpu.VMEM(rows.shape, jnp.bfloat16),
            pltpu.SemaphoreType.DMA((FETCHES + 1,)),
        ],
        compiler_params=limit(8),
        name="box_sums",
    )(counts, near(after), far(tag), far(rows))


def deal_kernel(keep_ref, got_ref, out_ref):
    for y in range(ALONG):
        for x in range(ALONG):
            for z in range(ALONG):
                i = (y * ALONG + x) * ALONG + z
                total = keep_ref[i].astype(jnp.float32) + got_ref[i].astype(jnp.float32)
                out_ref[y * ALONG + z, x] = total.astype(jnp.bfloat16)


def deal(keep, got):
    return kernel_call(
        deal_kernel,
        in_specs=[VMEM] * 2,
        out_specs=VMEM,
        out_shape=pltpu.VMEM((ALONG * ALONG, ALONG, BOXES, WIDTH), jnp.bfloat16),
        compiler_params=limit(4),
        name="deal",
    )(near(keep), near(got))


def add_kernel(parts_ref, out_ref):
    out_ref[...] = sum(parts_ref[i].astype(jnp.float32) for i in range(parts_ref.shape[0]))


def add(parts):
    return kernel_call(
        add_kernel,
        in_specs=[VMEM],
        out_specs=VMEM,
        out_shape=pltpu.VMEM(parts.shape[1:], jnp.float32),
        compiler_params=limit(4),
        name="add",
    )(near(parts))


def expand_kernel(after_ref, map_ref, *refs):
    parts, (mine_ref, other_ref) = refs[:-2], refs[-2:]
    place = place_of("x")
    for there, out_ref in ((place, mine_ref), (jnp.bitwise_xor(place, 1), other_ref)):
        total = sum(p[there] for p in parts).astype(jnp.bfloat16)
        out_ref[...] = jnp.dot(total, map_ref[...], preferred_element_type=jnp.float32)


def expand(after, source_map, parts):
    return kernel_call(
        expand_kernel,
        in_specs=[ANY] + [VMEM] * (1 + len(parts)),
        out_specs=[VMEM] * 2,
        out_shape=[pltpu.VMEM((BOXES, WIDTH), jnp.float32)] * 2,
        compiler_params=limit(4),
        name="expand",
    )(near(after), near(source_map), *map(near, parts))


def mats_kernel(after_ref, trans_ref, *out_refs):
    for level, out_ref in enumerate(out_refs):
        place = place_of(("x", "core", "x", "z")[level])
        pair = trans_ref[level, lax.rem(lax.div(place, jnp.int32(1 + (level == 2))), jnp.int32(2))]
        out_ref[:, :WIDTH] = pair[0].T
        out_ref[:, WIDTH:] = pair[1].T


def pick_mats(after, trans):
    return kernel_call(
        mats_kernel,
        in_specs=[ANY, VMEM],
        out_specs=[VMEM] * LEVELS,
        out_shape=[pltpu.VMEM((WIDTH, 2 * WIDTH), jnp.bfloat16)] * LEVELS,
        compiler_params=limit(4),
        name="mats",
    )(near(after), near(trans))


def column(x_ref, box):
    row = jnp.broadcast_to(x_ref[box : box + 1, :], (8, WIDTH))
    return row.T[:, :1]


def first_kernel(start, boxes, x_ref, other_x_ref, mats_ref, phases_ref, other_ref, *rest):
    out_ref = rest[-1]
    per = min(boxes, SPAN // DIRS)
    for b in range(0, boxes, per):
        both = []
        for box in range(start + b, start + b + per):
            cols = pl.ds(box * DIRS, DIRS)
            mine = column(x_ref, box)
            state = turn(mine[:HALF], mine[HALF:], *cos_sin(phases_ref[0, :, cols]))
            theirs = column(other_x_ref, box)
            angle = other_ref[:, cols].astype(jnp.int32).astype(jnp.float32) * (1.0 / TURN)
            partner = turn(theirs[:HALF], theirs[HALF:], *cos_sin(angle))
            both.append(jnp.concatenate([state, partner], axis=0))
        mixed = jnp.dot(mats_ref[...], jnp.concatenate(both, axis=1), preferred_element_type=jnp.float32)
        cols = pl.ds((start + b) * DIRS, per * DIRS)
        out_ref[:, b * DIRS : (b + per) * DIRS] = turn(mixed[:HALF], mixed[HALF:], *cos_sin(phases_ref[1, :, cols]))


def first_level(start, boxes, x, other_x, mats, phases, others, after):
    return kernel_call(
        functools.partial(first_kernel, start, boxes),
        in_specs=[VMEM] * 5 + [ANY] * len(after),
        out_specs=VMEM,
        out_shape=pltpu.VMEM((WIDTH, boxes * DIRS), jnp.bfloat16),
        compiler_params=limit(8),
        flops=FLOPS,
        name="a_%d" % start,
    )(near(x), near(other_x), near(mats), near(phases), near(others), *map(near, after))


def mix(start, skip, slot, cols, state_ref, partner_ref, mats_ref, phases_ref):
    here = pl.ds((start - skip) * DIRS + cols.start, cols.size)
    there = pl.ds(start * DIRS + cols.start, cols.size)
    both = jnp.concatenate([state_ref[:, here], partner_ref[:, here]], axis=0)
    mixed = jnp.dot(mats_ref[...], both, preferred_element_type=jnp.float32)
    return turn(mixed[:HALF], mixed[HALF:], *cos_sin(phases_ref[slot, :, there]))


def spans(boxes):
    size = min(boxes * DIRS, SPAN)
    return [pl.ds(b, size) for b in range(0, boxes * DIRS, size)]


def level_kernel(start, boxes, skip, slot, state_ref, partner_ref, mats_ref, phases_ref, *rest):
    out_ref = rest[-1]
    for cols in spans(boxes):
        out_ref[:, cols] = mix(start, skip, slot, cols, state_ref, partner_ref, mats_ref, phases_ref)


def next_level(name, start, boxes, skip, slot, state, partner, mats, phases, after):
    return kernel_call(
        functools.partial(level_kernel, start, boxes, skip, slot),
        in_specs=[VMEM] * 4 + [ANY] * len(after),
        out_specs=VMEM,
        out_shape=pltpu.VMEM((WIDTH, boxes * DIRS), jnp.bfloat16),
        compiler_params=limit(8),
        flops=FLOPS,
        name="%s_%d" % (name, start),
    )(near(state), near(partner), near(mats), near(phases), *map(near, after))


def flush_kernel(*refs):
    parts, out_ref, sems = refs[:-2], refs[-2], refs[-1]
    copies, at = [], 0
    for i, part in enumerate(parts):
        size = part.shape[1]
        copies.append(pltpu.make_async_copy(part, out_ref.at[:, pl.ds(at, size)], sems.at[i]))
        copies[-1].start()
        at += size
    for copy in copies:
        copy.wait()


def flush(parts):
    return kernel_call(
        flush_kernel,
        in_specs=[VMEM] * len(parts),
        out_specs=ANY,
        out_shape=jax.ShapeDtypeStruct((WIDTH, ROWS), jnp.bfloat16),
        scratch_shapes=[pltpu.SemaphoreType.DMA((len(parts),))],
        compiler_params=limit(2),
        flops=FLOPS,
        name="flush",
    )(*map(near, parts))


def last_kernel(start, boxes, slot, state_ref, partner_ref, mats_ref, phases_ref, before_ref, out_ref, held, sems):
    copies = []
    for i, cols in enumerate(spans(boxes)):
        held[:, cols] = mix(start, start, slot, cols, state_ref, partner_ref, mats_ref, phases_ref)
        there = pl.ds(start * DIRS + cols.start, cols.size)
        copies.append(pltpu.make_async_copy(held.at[:, cols], out_ref.at[:, there], sems.at[i]))
        copies[-1].start()
    for copy in copies:
        copy.wait()


def last_level(start, boxes, slot, state, partner, mats, phases, before):
    return kernel_call(
        functools.partial(last_kernel, start, boxes, slot),
        in_specs=[VMEM] * 4 + [ANY],
        out_specs=ANY,
        out_shape=jax.ShapeDtypeStruct((WIDTH, ROWS), jnp.bfloat16),
        input_output_aliases={4: 0},
        scratch_shapes=[
            pltpu.VMEM((WIDTH, boxes * DIRS), jnp.bfloat16),
            pltpu.SemaphoreType.DMA((len(spans(boxes)),)),
        ],
        compiler_params=limit(8),
        flops=FLOPS,
        name="last",
    )(near(state), near(partner), near(mats), near(phases), far(before))


def move(value, axis, mask):
    return lax.ppermute(value, axis, [(s, s ^ mask) for s in range(lax.axis_size(axis))])


def per_device(currents, counts, box_of, source_map, phases, trans):
    turns = encode(phases)
    others = move(turns, "bx", 1)
    keep, send = box_sums(counts, turns, box_of[0], currents[0])
    got = move(send, "by", 1)
    plane = [
        [(y * ALONG + x) * 2 * ALONG + z * 2 + core for y in range(ALONG) for z in range(ALONG)]
        for x in range(ALONG)
        for core in range(2)
    ]
    parts = lax.all_to_all(
        deal(keep, got), ("bx", "by"), split_axis=0, concat_axis=0, tiled=True, axis_index_groups=plane
    )
    row = add(parts)
    early = phases[0:3]
    mats = pick_mats(row, trans)
    mine, theirs = expand(mats[0], source_map, [row] + [move(row, "bx", k) for k in (1, 2, 3)])

    starts = [sum(PARTS[:i]) for i in range(len(PARTS))]
    groups = [range(sum(GROUPS[:g]), sum(GROUPS[: g + 1])) for g in range(len(GROUPS))]
    final = len(PARTS) - 1
    firsts, states, partners, out = {}, {}, {}, None
    after = []
    for name in ORDER.split():
        if name == "f":
            late = phases[3:5]
            continue
        level, i = name[0], int(name[1:])
        if level == "a":
            start, boxes = starts[groups[i][0]], sum(PARTS[p] for p in groups[i])
            done = first_level(start, boxes, mine, theirs, mats[0], early, others, after)
            swapped = move(done, "by", 1)
            for p in groups[i]:
                firsts[p] = (start, done, swapped)
        elif level == "b":
            skip, value, other = firsts[i]
            done = next_level(level, starts[i], PARTS[i], skip, 2, value, other, mats[1], early, after)
            states[i], partners[i] = done, move(done, "bx", 2)
        elif level == "c":
            ends = (starts[i], PARTS[i], starts[i], 0)
            done = next_level(level, *ends, states[i], partners[i], mats[2], late, after)
            states[i], partners[i] = done, move(done, "by", 2)
        elif i < final:
            ends = (starts[i], PARTS[i], starts[i], 1)
            done = next_level(level, *ends, states[i], partners[i], mats[3], late, after)
            states[i] = done
        else:
            out = flush([states[p] for p in range(final)])
            return last_level(starts[i], PARTS[i], 1, states[i], partners[i], mats[3], late, out)
        after = [done]


def solution(mesh):
    placed = (
        P(("bx", "by"), None, None, None),
        P(("bx", "by"), None),
        P(("bx", "by"), None, None),
        P(),
        P(None, None, ("bx", "by")),
        P(),
    )
    return jax.shard_map(
        per_device, mesh=mesh, in_specs=placed, out_specs=P(None, ("bx", "by")), check_vma=False
    )
```

```python
import functools

import jax
import jax.numpy as jnp
from jax import lax
from jax.experimental import pallas as pl
from jax.experimental.pallas import tpu as pltpu
from jax.sharding import PartitionSpec as P

BOXES = 16
DIRS = 512
HALF = 64
WIDTH = 128
ROWS = BOXES * DIRS
LEVELS = 4
PARTS = (2, 2, 2, 2, 2, 2, 2, 1, 1)
GROUPS = (1, 1, 2, 2, 3)
ORDER = (
    "a0", "a1", "b0", "a2", "b1", "b2", "c0", "a3", "b3",
    "c1", "b4", "c2", "d0", "a4", "b5", "c3", "d1", "b6",
    "c4", "d2", "b7", "c5", "b8", "d3", "c6", "d4", "c7",
    "d5", "c8", "d6", "d7", "d8",
)
SPAN = 1024
FETCHES = 4
ALONG = 4
FLOPS = 10**10
MIB = 1 << 20

TURN = 32767.0 / 3.141592653589793
SIN_HALF = (0.7071043848991394, -0.02945953793823719, 0.0003670926089398563, -2.0290131033107173e-06)
COS_HALF = (
    1.4142135381698608,
    -0.17677636444568634,
    0.003682575887069106,
    -3.061274401261471e-05,
    1.2791403491974052e-07,
)

ANY = pl.BlockSpec(memory_space=pl.ANY)
VMEM = pl.BlockSpec(memory_space=pltpu.VMEM)
SMEM = pl.BlockSpec(memory_space=pltpu.SMEM)


def near(value):
    return pltpu.with_memory_space_constraint(value, pltpu.VMEM)


def far(value):
    return pltpu.with_memory_space_constraint(value, pltpu.HBM)


def limit(mib):
    return pltpu.CompilerParams(vmem_limit_bytes=mib * MIB)


def kernel_call(*args, flops=1000, **kwargs):
    cost = pl.CostEstimate(flops=flops, bytes_accessed=1000, transcendentals=0)
    return pl.pallas_call(*args, cost_estimate=cost, **kwargs)


def place_of(part):
    axis, shift, count = {"core": ("by", 0, 2), "z": ("by", 1, 4), "x": ("bx", 0, 4), "y": ("bx", 2, 4)}[part]
    return lax.rem(lax.div(lax.axis_index(axis).astype(jnp.int32), jnp.int32(1 << shift)), jnp.int32(count))


def horner(terms, square):
    total = jnp.full_like(square, terms[-1])
    for term in terms[-2::-1]:
        total = total * square + term
    return total


def cos_sin(angle):
    square = angle * angle
    sine = horner(SIN_HALF, square) * angle
    cosine = horner(COS_HALF, square)
    return 1.0 - sine * sine, sine * cosine


def turn(re, im, cosine, sine):
    top = re * cosine - im * sine
    low = re * sine + im * cosine
    return jnp.concatenate([top, low], axis=0).astype(jnp.bfloat16)


def encode_kernel(phases_ref, out_ref, held, sems):
    span = ROWS // FETCHES
    copies = []
    for i in range(FETCHES):
        cols = pl.ds(i * span, span)
        copies.append(pltpu.make_async_copy(phases_ref.at[0, :, cols], held.at[:, cols], sems.at[i]))
        copies[-1].start()
    for i in range(FETCHES):
        copies[i].wait()
        cols = pl.ds(i * span, span)
        out_ref[:, cols] = jnp.round(held[:, cols] * TURN).astype(jnp.int32).astype(jnp.int16)


def encode(phases):
    return kernel_call(
        encode_kernel,
        in_specs=[ANY],
        out_specs=VMEM,
        out_shape=pltpu.VMEM((HALF, ROWS), jnp.int16),
        scratch_shapes=[pltpu.VMEM((HALF, ROWS), jnp.float32), pltpu.SemaphoreType.DMA((FETCHES,))],
        compiler_params=limit(8),
        name="encode",
    )(far(phases))


def box_sums_kernel(counts_ref, after_ref, tag_hbm_ref, rows_ref, keep_ref, send_ref, tag_ref, held, sems):
    step = WIDTH // FETCHES
    tags = pltpu.make_async_copy(tag_hbm_ref, tag_ref, sems.at[FETCHES])
    tags.start()
    copies = []
    for i in range(FETCHES):
        some = pl.ds(i * step, step)
        copies.append(pltpu.make_async_copy(rows_ref.at[some], held.at[some], sems.at[i]))
        copies[-1].start()
    tags.wait()
    slot = lax.broadcasted_iota(jnp.int32, (BOXES, WIDTH), 1)
    label = lax.broadcasted_iota(jnp.int32, (BOXES, WIDTH), 0)
    first = place_of("core") == 0

    def picks(j):
        hit = jnp.logical_and(tag_ref[j : j + 1, :] == label, slot < counts_ref[0, j])
        return jnp.where(hit, 1.0, 0.0).astype(jnp.bfloat16)

    for i in range(FETCHES):
        copies[i].wait()
        for j in range(i * step, (i + 1) * step, 2):
            left = jnp.concatenate([picks(j), picks(j + 1)], axis=0)
            right = jnp.concatenate([held[j], held[j + 1]], axis=1)
            sums = jnp.dot(left, right, preferred_element_type=jnp.float32)
            even, odd = sums[:BOXES, :WIDTH], sums[BOXES:, WIDTH:]
            keep_ref[j // 2] = jnp.where(first, even, odd).astype(jnp.bfloat16)
            send_ref[j // 2] = jnp.where(first, odd, even).astype(jnp.bfloat16)


def box_sums(counts, after, tag, rows):
    owners = rows.shape[0]
    return kernel_call(
        box_sums_kernel,
        in_specs=[SMEM, ANY, ANY, ANY],
        out_specs=[VMEM] * 2,
        out_shape=[pltpu.VMEM((owners // 2, BOXES, WIDTH), jnp.bfloat16)] * 2,
        scratch_shapes=[
            pltpu.VMEM(tag.shape, jnp.int32),
            pltpu.VMEM(rows.shape, jnp.bfloat16),
            pltpu.SemaphoreType.DMA((FETCHES + 1,)),
        ],
        compiler_params=limit(8),
        name="box_sums",
    )(counts, near(after), far(tag), far(rows))


def deal_kernel(keep_ref, got_ref, out_ref):
    for y in range(ALONG):
        for x in range(ALONG):
            for z in range(ALONG):
                i = (y * ALONG + x) * ALONG + z
                total = keep_ref[i].astype(jnp.float32) + got_ref[i].astype(jnp.float32)
                out_ref[y * ALONG + z, x] = total.astype(jnp.bfloat16)


def deal(keep, got):
    return kernel_call(
        deal_kernel,
        in_specs=[VMEM] * 2,
        out_specs=VMEM,
        out_shape=pltpu.VMEM((ALONG * ALONG, ALONG, BOXES, WIDTH), jnp.bfloat16),
        compiler_params=limit(4),
        name="deal",
    )(near(keep), near(got))


def add_kernel(parts_ref, out_ref):
    out_ref[...] = sum(parts_ref[i].astype(jnp.float32) for i in range(parts_ref.shape[0]))


def add(parts):
    return kernel_call(
        add_kernel,
        in_specs=[VMEM],
        out_specs=VMEM,
        out_shape=pltpu.VMEM(parts.shape[1:], jnp.float32),
        compiler_params=limit(4),
        name="add",
    )(near(parts))


def expand_kernel(after_ref, map_ref, *refs):
    parts, (mine_ref, other_ref) = refs[:-2], refs[-2:]
    place = place_of("x")
    for there, out_ref in ((place, mine_ref), (jnp.bitwise_xor(place, 1), other_ref)):
        total = sum(p[there] for p in parts).astype(jnp.bfloat16)
        out_ref[...] = jnp.dot(total, map_ref[...], preferred_element_type=jnp.float32)


def expand(after, source_map, parts):
    return kernel_call(
        expand_kernel,
        in_specs=[ANY] + [VMEM] * (1 + len(parts)),
        out_specs=[VMEM] * 2,
        out_shape=[pltpu.VMEM((BOXES, WIDTH), jnp.float32)] * 2,
        compiler_params=limit(4),
        name="expand",
    )(near(after), near(source_map), *map(near, parts))


def mats_kernel(after_ref, trans_ref, *out_refs):
    for level, out_ref in enumerate(out_refs):
        place = place_of(("x", "core", "x", "z")[level])
        pair = trans_ref[level, lax.rem(lax.div(place, jnp.int32(1 + (level == 2))), jnp.int32(2))]
        out_ref[:, :WIDTH] = pair[0].T
        out_ref[:, WIDTH:] = pair[1].T


def pick_mats(after, trans):
    return kernel_call(
        mats_kernel,
        in_specs=[ANY, VMEM],
        out_specs=[VMEM] * LEVELS,
        out_shape=[pltpu.VMEM((WIDTH, 2 * WIDTH), jnp.bfloat16)] * LEVELS,
        compiler_params=limit(4),
        name="mats",
    )(near(after), near(trans))


def column(x_ref, box):
    row = jnp.broadcast_to(x_ref[box : box + 1, :], (8, WIDTH))
    return row.T[:, :1]


def first_kernel(start, boxes, x_ref, other_x_ref, mats_ref, phases_ref, other_ref, *rest):
    out_ref = rest[-1]
    per = min(boxes, SPAN // DIRS)
    for b in range(0, boxes, per):
        both = []
        for box in range(start + b, start + b + per):
            cols = pl.ds(box * DIRS, DIRS)
            mine = column(x_ref, box)
            state = turn(mine[:HALF], mine[HALF:], *cos_sin(phases_ref[0, :, cols]))
            theirs = column(other_x_ref, box)
            angle = other_ref[:, cols].astype(jnp.int32).astype(jnp.float32) * (1.0 / TURN)
            partner = turn(theirs[:HALF], theirs[HALF:], *cos_sin(angle))
            both.append(jnp.concatenate([state, partner], axis=0))
        mixed = jnp.dot(mats_ref[...], jnp.concatenate(both, axis=1), preferred_element_type=jnp.float32)
        cols = pl.ds((start + b) * DIRS, per * DIRS)
        out_ref[:, b * DIRS : (b + per) * DIRS] = turn(mixed[:HALF], mixed[HALF:], *cos_sin(phases_ref[1, :, cols]))


def first_level(start, boxes, x, other_x, mats, phases, others, after):
    return kernel_call(
        functools.partial(first_kernel, start, boxes),
        in_specs=[VMEM] * 5 + [ANY] * len(after),
        out_specs=VMEM,
        out_shape=pltpu.VMEM((WIDTH, boxes * DIRS), jnp.bfloat16),
        compiler_params=limit(8),
        flops=FLOPS,
        name="a_%d" % start,
    )(near(x), near(other_x), near(mats), near(phases), near(others), *map(near, after))


def mix(start, skip, slot, cols, state_ref, partner_ref, mats_ref, phases_ref):
    here = pl.ds((start - skip) * DIRS + cols.start, cols.size)
    there = pl.ds(start * DIRS + cols.start, cols.size)
    both = jnp.concatenate([state_ref[:, here], partner_ref[:, here]], axis=0)
    mixed = jnp.dot(mats_ref[...], both, preferred_element_type=jnp.float32)
    return turn(mixed[:HALF], mixed[HALF:], *cos_sin(phases_ref[slot, :, there]))


def spans(boxes):
    size = min(boxes * DIRS, SPAN)
    return [pl.ds(b, size) for b in range(0, boxes * DIRS, size)]


def level_kernel(start, boxes, skip, slot, state_ref, partner_ref, mats_ref, phases_ref, *rest):
    out_ref = rest[-1]
    for cols in spans(boxes):
        out_ref[:, cols] = mix(start, skip, slot, cols, state_ref, partner_ref, mats_ref, phases_ref)


def next_level(name, start, boxes, skip, slot, state, partner, mats, phases, after):
    return kernel_call(
        functools.partial(level_kernel, start, boxes, skip, slot),
        in_specs=[VMEM] * 4 + [ANY] * len(after),
        out_specs=VMEM,
        out_shape=pltpu.VMEM((WIDTH, boxes * DIRS), jnp.bfloat16),
        compiler_params=limit(8),
        flops=FLOPS,
        name="%s_%d" % (name, start),
    )(near(state), near(partner), near(mats), near(phases), *map(near, after))


def flush_kernel(*refs):
    parts, out_ref, sems = refs[:-2], refs[-2], refs[-1]
    copies, at = [], 0
    for i, part in enumerate(parts):
        size = part.shape[1]
        copies.append(pltpu.make_async_copy(part, out_ref.at[:, pl.ds(at, size)], sems.at[i]))
        copies[-1].start()
        at += size
    for copy in copies:
        copy.wait()


def flush(parts):
    return kernel_call(
        flush_kernel,
        in_specs=[VMEM] * len(parts),
        out_specs=ANY,
        out_shape=jax.ShapeDtypeStruct((WIDTH, ROWS), jnp.bfloat16),
        scratch_shapes=[pltpu.SemaphoreType.DMA((len(parts),))],
        compiler_params=limit(2),
        flops=FLOPS,
        name="flush",
    )(*map(near, parts))


def last_kernel(start, boxes, slot, state_ref, partner_ref, mats_ref, phases_ref, before_ref, out_ref, held, sems):
    copies = []
    for i, cols in enumerate(spans(boxes)):
        held[:, cols] = mix(start, start, slot, cols, state_ref, partner_ref, mats_ref, phases_ref)
        there = pl.ds(start * DIRS + cols.start, cols.size)
        copies.append(pltpu.make_async_copy(held.at[:, cols], out_ref.at[:, there], sems.at[i]))
        copies[-1].start()
    for copy in copies:
        copy.wait()


def last_level(start, boxes, slot, state, partner, mats, phases, before):
    return kernel_call(
        functools.partial(last_kernel, start, boxes, slot),
        in_specs=[VMEM] * 4 + [ANY],
        out_specs=ANY,
        out_shape=jax.ShapeDtypeStruct((WIDTH, ROWS), jnp.bfloat16),
        input_output_aliases={4: 0},
        scratch_shapes=[
            pltpu.VMEM((WIDTH, boxes * DIRS), jnp.bfloat16),
            pltpu.SemaphoreType.DMA((len(spans(boxes)),)),
        ],
        compiler_params=limit(8),
        flops=FLOPS,
        name="last_%d" % start,
    )(near(state), near(partner), near(mats), near(phases), far(before))


def move(value, axis, mask):
    return lax.ppermute(value, axis, [(s, s ^ mask) for s in range(lax.axis_size(axis))])


def per_device(currents, counts, box_of, source_map, phases, trans):
    turns = encode(phases)
    others = move(turns, "bx", 1)
    keep, send = box_sums(counts, turns, box_of[0], currents[0])
    got = move(send, "by", 1)
    plane = [
        [(y * ALONG + x) * 2 * ALONG + z * 2 + core for y in range(ALONG) for z in range(ALONG)]
        for x in range(ALONG)
        for core in range(2)
    ]
    parts = lax.all_to_all(
        deal(keep, got), ("bx", "by"), split_axis=0, concat_axis=0, tiled=True, axis_index_groups=plane
    )
    row = add(parts)
    mats = pick_mats(row, trans)
    mine, theirs = expand(mats[0], source_map, [row] + [move(row, "bx", k) for k in (1, 2, 3)])

    starts = [sum(PARTS[:i]) for i in range(len(PARTS))]
    groups = [range(sum(GROUPS[:g]), sum(GROUPS[: g + 1])) for g in range(len(GROUPS))]
    flushed = len(PARTS) - 2
    firsts, states, partners, out = {}, {}, {}, None
    after = []
    for name in ORDER:
        level, i = name[0], int(name[1:])
        if level == "a":
            start, boxes = starts[groups[i][0]], sum(PARTS[p] for p in groups[i])
            done = first_level(start, boxes, mine, theirs, mats[0], phases, others, after)
            swapped = move(done, "by", 1)
            for p in groups[i]:
                firsts[p] = (start, done, swapped)
        elif level == "b":
            skip, value, other = firsts[i]
            done = next_level(level, starts[i], PARTS[i], skip, 2, value, other, mats[1], phases, after)
            states[i], partners[i] = done, move(done, "bx", 2)
        elif level == "c":
            ends = (starts[i], PARTS[i], starts[i], 3)
            done = next_level(level, *ends, states[i], partners[i], mats[2], phases, after)
            states[i], partners[i] = done, move(done, "by", 2)
        elif i < flushed:
            ends = (starts[i], PARTS[i], starts[i], 4)
            done = next_level(level, *ends, states[i], partners[i], mats[3], phases, after)
            states[i] = done
        else:
            if out is None:
                out = flush([states[p] for p in range(flushed)])
            out = last_level(starts[i], PARTS[i], 4, states[i], partners[i], mats[3], phases, out)
            continue
        after = [done]
    return out


def solution(mesh):
    placed = (
        P(("bx", "by"), None, None, None),
        P(("bx", "by"), None),
        P(("bx", "by"), None, None),
        P(),
        P(None, None, ("bx", "by")),
        P(),
    )
    return jax.shard_map(
        per_device, mesh=mesh, in_specs=placed, out_specs=P(None, ("bx", "by")), check_vma=False
    )
```

```python
import functools

import jax
import jax.numpy as jnp
from jax import lax
from jax.experimental import pallas as pl
from jax.experimental.pallas import tpu as pltpu
from jax.sharding import PartitionSpec as P

BOXES = 16
DIRS = 512
HALF = 64
WIDTH = 128
ROWS = BOXES * DIRS
LEVELS = 4
PARTS = (2, 2, 2, 2, 2, 2, 2, 1, 1)
GROUPS = (1, 1, 2, 2, 3)
ORDER = (
    "a0", "a1", "b0", "a2", "b1", "b2", "c0", "a3", "b3",
    "c1", "b4", "c2", "d0", "a4", "b5", "c3", "d1", "b6",
    "c4", "d2", "b7", "c5", "b8", "d3", "c6", "d4", "c7",
    "d5", "c8", "d6", "d7", "d8",
)
SPAN = 1024
FETCHES = 4
ALONG = 4
FLOPS = 10**10
MIB = 1 << 20

TURN = 32767.0 / 3.141592653589793
SIN_HALF = (0.7071043848991394, -0.02945953793823719, 0.0003670926089398563, -2.0290131033107173e-06)
COS_HALF = (
    1.4142135381698608,
    -0.17677636444568634,
    0.003682575887069106,
    -3.061274401261471e-05,
    1.2791403491974052e-07,
)

ANY = pl.BlockSpec(memory_space=pl.ANY)
VMEM = pl.BlockSpec(memory_space=pltpu.VMEM)
SMEM = pl.BlockSpec(memory_space=pltpu.SMEM)


def near(value):
    return pltpu.with_memory_space_constraint(value, pltpu.VMEM)


def far(value):
    return pltpu.with_memory_space_constraint(value, pltpu.HBM)


def limit(mib):
    return pltpu.CompilerParams(vmem_limit_bytes=mib * MIB)


def kernel_call(*args, flops=1000, **kwargs):
    cost = pl.CostEstimate(flops=flops, bytes_accessed=1000, transcendentals=0)
    return pl.pallas_call(*args, cost_estimate=cost, **kwargs)


def place_of(part):
    axis, shift, count = {"core": ("by", 0, 2), "z": ("by", 1, 4), "x": ("bx", 0, 4), "y": ("bx", 2, 4)}[part]
    return lax.rem(lax.div(lax.axis_index(axis).astype(jnp.int32), jnp.int32(1 << shift)), jnp.int32(count))


def horner(terms, square):
    total = jnp.full_like(square, terms[-1])
    for term in terms[-2::-1]:
        total = total * square + term
    return total


def cos_sin(angle):
    square = angle * angle
    sine = horner(SIN_HALF, square) * angle
    cosine = horner(COS_HALF, square)
    return 1.0 - sine * sine, sine * cosine


def turn(re, im, cosine, sine):
    top = re * cosine - im * sine
    low = re * sine + im * cosine
    return jnp.concatenate([top, low], axis=0).astype(jnp.bfloat16)


def encode_kernel(phases_ref, out_ref, held, sems):
    span = ROWS // FETCHES
    copies = []
    for i in range(FETCHES):
        cols = pl.ds(i * span, span)
        copies.append(pltpu.make_async_copy(phases_ref.at[0, :, cols], held.at[:, cols], sems.at[i]))
        copies[-1].start()
    for i in range(FETCHES):
        copies[i].wait()
        cols = pl.ds(i * span, span)
        out_ref[:, cols] = jnp.round(held[:, cols] * TURN).astype(jnp.int32).astype(jnp.int16)


def encode(phases):
    return kernel_call(
        encode_kernel,
        in_specs=[ANY],
        out_specs=VMEM,
        out_shape=pltpu.VMEM((HALF, ROWS), jnp.int16),
        scratch_shapes=[pltpu.VMEM((HALF, ROWS), jnp.float32), pltpu.SemaphoreType.DMA((FETCHES,))],
        compiler_params=limit(8),
        name="encode",
    )(far(phases))


def box_sums_kernel(counts_ref, after_ref, tag_hbm_ref, rows_ref, keep_ref, send_ref, tag_ref, held, sems):
    step = WIDTH // FETCHES
    tags = pltpu.make_async_copy(tag_hbm_ref, tag_ref, sems.at[FETCHES])
    tags.start()
    copies = []
    for i in range(FETCHES):
        some = pl.ds(i * step, step)
        copies.append(pltpu.make_async_copy(rows_ref.at[some], held.at[some], sems.at[i]))
        copies[-1].start()
    tags.wait()
    slot = lax.broadcasted_iota(jnp.int32, (BOXES, WIDTH), 1)
    label = lax.broadcasted_iota(jnp.int32, (BOXES, WIDTH), 0)
    first = place_of("core") == 0

    def picks(j):
        hit = jnp.logical_and(tag_ref[j : j + 1, :] == label, slot < counts_ref[0, j])
        return jnp.where(hit, 1.0, 0.0).astype(jnp.bfloat16)

    for i in range(FETCHES):
        copies[i].wait()
        for j in range(i * step, (i + 1) * step, 2):
            left = jnp.concatenate([picks(j), picks(j + 1)], axis=0)
            right = jnp.concatenate([held[j], held[j + 1]], axis=1)
            sums = jnp.dot(left, right, preferred_element_type=jnp.float32)
            even, odd = sums[:BOXES, :WIDTH], sums[BOXES:, WIDTH:]
            keep_ref[j // 2] = jnp.where(first, even, odd).astype(jnp.bfloat16)
            send_ref[j // 2] = jnp.where(first, odd, even).astype(jnp.bfloat16)


def box_sums(counts, after, tag, rows):
    owners = rows.shape[0]
    return kernel_call(
        box_sums_kernel,
        in_specs=[SMEM, ANY, ANY, ANY],
        out_specs=[VMEM] * 2,
        out_shape=[pltpu.VMEM((owners // 2, BOXES, WIDTH), jnp.bfloat16)] * 2,
        scratch_shapes=[
            pltpu.VMEM(tag.shape, jnp.int32),
            pltpu.VMEM(rows.shape, jnp.bfloat16),
            pltpu.SemaphoreType.DMA((FETCHES + 1,)),
        ],
        compiler_params=limit(8),
        name="box_sums",
    )(counts, near(after), far(tag), far(rows))


def deal_kernel(keep_ref, got_ref, out_ref):
    for y in range(ALONG):
        for x in range(ALONG):
            for z in range(ALONG):
                i = (y * ALONG + x) * ALONG + z
                total = keep_ref[i].astype(jnp.float32) + got_ref[i].astype(jnp.float32)
                out_ref[y * ALONG + z, x] = total.astype(jnp.bfloat16)


def deal(keep, got):
    return kernel_call(
        deal_kernel,
        in_specs=[VMEM] * 2,
        out_specs=VMEM,
        out_shape=pltpu.VMEM((ALONG * ALONG, ALONG, BOXES, WIDTH), jnp.bfloat16),
        compiler_params=limit(4),
        name="deal",
    )(near(keep), near(got))


def add_kernel(parts_ref, out_ref, sent_ref):
    total = sum(parts_ref[i].astype(jnp.float32) for i in range(parts_ref.shape[0]))
    out_ref[...] = total
    sent_ref[...] = total.astype(jnp.bfloat16)


def add(parts):
    return kernel_call(
        add_kernel,
        in_specs=[VMEM],
        out_specs=[VMEM] * 2,
        out_shape=[pltpu.VMEM(parts.shape[1:], kind) for kind in (jnp.float32, jnp.bfloat16)],
        compiler_params=limit(4),
        name="add",
    )(near(parts))


def expand_kernel(after_ref, map_ref, *refs):
    parts, (mine_ref, other_ref) = refs[:-2], refs[-2:]
    place = place_of("x")
    for there, out_ref in ((place, mine_ref), (jnp.bitwise_xor(place, 1), other_ref)):
        total = sum(p[there].astype(jnp.float32) for p in parts).astype(jnp.bfloat16)
        out_ref[...] = jnp.dot(total, map_ref[...], preferred_element_type=jnp.float32)


def expand(after, source_map, parts):
    return kernel_call(
        expand_kernel,
        in_specs=[ANY] + [VMEM] * (1 + len(parts)),
        out_specs=[VMEM] * 2,
        out_shape=[pltpu.VMEM((BOXES, WIDTH), jnp.float32)] * 2,
        compiler_params=limit(4),
        name="expand",
    )(near(after), near(source_map), *map(near, parts))


def mats_kernel(after_ref, trans_ref, *out_refs):
    for level, out_ref in enumerate(out_refs):
        place = place_of(("x", "core", "x", "z")[level])
        pair = trans_ref[level, lax.rem(lax.div(place, jnp.int32(1 + (level == 2))), jnp.int32(2))]
        out_ref[:, :WIDTH] = pair[0].T
        out_ref[:, WIDTH:] = pair[1].T


def pick_mats(after, trans):
    return kernel_call(
        mats_kernel,
        in_specs=[ANY, VMEM],
        out_specs=[VMEM] * LEVELS,
        out_shape=[pltpu.VMEM((WIDTH, 2 * WIDTH), jnp.bfloat16)] * LEVELS,
        compiler_params=limit(4),
        name="mats",
    )(near(after), near(trans))


def column(x_ref, box):
    row = jnp.broadcast_to(x_ref[box : box + 1, :], (8, WIDTH))
    return row.T[:, :1]


def first_kernel(start, boxes, x_ref, other_x_ref, mats_ref, phases_ref, other_ref, *rest):
    out_ref = rest[-1]
    per = min(boxes, SPAN // DIRS)
    for b in range(0, boxes, per):
        both = []
        for box in range(start + b, start + b + per):
            cols = pl.ds(box * DIRS, DIRS)
            mine = column(x_ref, box)
            state = turn(mine[:HALF], mine[HALF:], *cos_sin(phases_ref[0, :, cols]))
            theirs = column(other_x_ref, box)
            angle = other_ref[:, cols].astype(jnp.int32).astype(jnp.float32) * (1.0 / TURN)
            partner = turn(theirs[:HALF], theirs[HALF:], *cos_sin(angle))
            both.append(jnp.concatenate([state, partner], axis=0))
        mixed = jnp.dot(mats_ref[...], jnp.concatenate(both, axis=1), preferred_element_type=jnp.float32)
        cols = pl.ds((start + b) * DIRS, per * DIRS)
        out_ref[:, b * DIRS : (b + per) * DIRS] = turn(mixed[:HALF], mixed[HALF:], *cos_sin(phases_ref[1, :, cols]))


def first_level(start, boxes, x, other_x, mats, phases, others, after):
    return kernel_call(
        functools.partial(first_kernel, start, boxes),
        in_specs=[VMEM] * 5 + [ANY] * len(after),
        out_specs=VMEM,
        out_shape=pltpu.VMEM((WIDTH, boxes * DIRS), jnp.bfloat16),
        compiler_params=limit(8),
        flops=FLOPS,
        name="a_%d" % start,
    )(near(x), near(other_x), near(mats), near(phases), near(others), *map(near, after))


def mix(start, skip, slot, cols, state_ref, partner_ref, mats_ref, phases_ref):
    here = pl.ds((start - skip) * DIRS + cols.start, cols.size)
    there = pl.ds(start * DIRS + cols.start, cols.size)
    both = jnp.concatenate([state_ref[:, here], partner_ref[:, here]], axis=0)
    mixed = jnp.dot(mats_ref[...], both, preferred_element_type=jnp.float32)
    return turn(mixed[:HALF], mixed[HALF:], *cos_sin(phases_ref[slot, :, there]))


def spans(boxes):
    size = min(boxes * DIRS, SPAN)
    return [pl.ds(b, size) for b in range(0, boxes * DIRS, size)]


def level_kernel(start, boxes, skip, slot, state_ref, partner_ref, mats_ref, phases_ref, *rest):
    out_ref = rest[-1]
    for cols in spans(boxes):
        out_ref[:, cols] = mix(start, skip, slot, cols, state_ref, partner_ref, mats_ref, phases_ref)


def next_level(name, start, boxes, skip, slot, state, partner, mats, phases, after):
    return kernel_call(
        functools.partial(level_kernel, start, boxes, skip, slot),
        in_specs=[VMEM] * 4 + [ANY] * len(after),
        out_specs=VMEM,
        out_shape=pltpu.VMEM((WIDTH, boxes * DIRS), jnp.bfloat16),
        compiler_params=limit(8),
        flops=FLOPS,
        name="%s_%d" % (name, start),
    )(near(state), near(partner), near(mats), near(phases), *map(near, after))


def flush_kernel(*refs):
    parts, out_ref, sems = refs[:-2], refs[-2], refs[-1]
    copies, at = [], 0
    for i, part in enumerate(parts):
        size = part.shape[1]
        copies.append(pltpu.make_async_copy(part, out_ref.at[:, pl.ds(at, size)], sems.at[i]))
        copies[-1].start()
        at += size
    for copy in copies:
        copy.wait()


def flush(parts):
    return kernel_call(
        flush_kernel,
        in_specs=[VMEM] * len(parts),
        out_specs=ANY,
        out_shape=jax.ShapeDtypeStruct((WIDTH, ROWS), jnp.bfloat16),
        scratch_shapes=[pltpu.SemaphoreType.DMA((len(parts),))],
        compiler_params=limit(2),
        flops=FLOPS,
        name="flush",
    )(*map(near, parts))


def last_kernel(start, boxes, slot, state_ref, partner_ref, mats_ref, phases_ref, before_ref, out_ref, held, sems):
    copies = []
    for i, cols in enumerate(spans(boxes)):
        held[:, cols] = mix(start, start, slot, cols, state_ref, partner_ref, mats_ref, phases_ref)
        there = pl.ds(start * DIRS + cols.start, cols.size)
        copies.append(pltpu.make_async_copy(held.at[:, cols], out_ref.at[:, there], sems.at[i]))
        copies[-1].start()
    for copy in copies:
        copy.wait()


def last_level(start, boxes, slot, state, partner, mats, phases, before):
    return kernel_call(
        functools.partial(last_kernel, start, boxes, slot),
        in_specs=[VMEM] * 4 + [ANY],
        out_specs=ANY,
        out_shape=jax.ShapeDtypeStruct((WIDTH, ROWS), jnp.bfloat16),
        input_output_aliases={4: 0},
        scratch_shapes=[
            pltpu.VMEM((WIDTH, boxes * DIRS), jnp.bfloat16),
            pltpu.SemaphoreType.DMA((len(spans(boxes)),)),
        ],
        compiler_params=limit(8),
        flops=FLOPS,
        name="last_%d" % start,
    )(near(state), near(partner), near(mats), near(phases), far(before))


def move(value, axis, mask):
    return lax.ppermute(value, axis, [(s, s ^ mask) for s in range(lax.axis_size(axis))])


def per_device(currents, counts, box_of, source_map, phases, trans):
    turns = encode(phases)
    others = move(turns, "bx", 1)
    keep, send = box_sums(counts, turns, box_of[0], currents[0])
    got = move(send, "by", 1)
    plane = [
        [(y * ALONG + x) * 2 * ALONG + z * 2 + core for y in range(ALONG) for z in range(ALONG)]
        for x in range(ALONG)
        for core in range(2)
    ]
    parts = lax.all_to_all(
        deal(keep, got), ("bx", "by"), split_axis=0, concat_axis=0, tiled=True, axis_index_groups=plane
    )
    row, sent = add(parts)
    mats = pick_mats(row, trans)
    mine, theirs = expand(mats[0], source_map, [row] + [move(sent, "bx", k) for k in (1, 2, 3)])

    starts = [sum(PARTS[:i]) for i in range(len(PARTS))]
    groups = [range(sum(GROUPS[:g]), sum(GROUPS[: g + 1])) for g in range(len(GROUPS))]
    flushed = len(PARTS) - 2
    firsts, states, partners, out = {}, {}, {}, None
    after = []
    for name in ORDER:
        level, i = name[0], int(name[1:])
        if level == "a":
            start, boxes = starts[groups[i][0]], sum(PARTS[p] for p in groups[i])
            done = first_level(start, boxes, mine, theirs, mats[0], phases, others, after)
            swapped = move(done, "by", 1)
            for p in groups[i]:
                firsts[p] = (start, done, swapped)
        elif level == "b":
            skip, value, other = firsts[i]
            done = next_level(level, starts[i], PARTS[i], skip, 2, value, other, mats[1], phases, after)
            states[i], partners[i] = done, move(done, "bx", 2)
        elif level == "c":
            ends = (starts[i], PARTS[i], starts[i], 3)
            done = next_level(level, *ends, states[i], partners[i], mats[2], phases, after)
            states[i], partners[i] = done, move(done, "by", 2)
        elif i < flushed:
            ends = (starts[i], PARTS[i], starts[i], 4)
            done = next_level(level, *ends, states[i], partners[i], mats[3], phases, after)
            states[i] = done
        else:
            if out is None:
                out = flush([states[p] for p in range(flushed)])
            out = last_level(starts[i], PARTS[i], 4, states[i], partners[i], mats[3], phases, out)
            continue
        after = [done]
    return out


def solution(mesh):
    placed = (
        P(("bx", "by"), None, None, None),
        P(("bx", "by"), None),
        P(("bx", "by"), None, None),
        P(),
        P(None, None, ("bx", "by")),
        P(),
    )
    return jax.shard_map(
        per_device, mesh=mesh, in_specs=placed, out_specs=P(None, ("bx", "by")), check_vma=False
    )
```
